256 devices in a mesh: real: 16 (over z_hi, y, core), sky: 16 (over z_lo, x).
Axes of the slice: x: 4, y: 4, z: 8 (z_hi: 2, z_lo: 4; z = z_hi * 4 + z_lo), core: 2. Of those that a mesh axis runs over, the one named last changes fastest.
Arguments:
- potential_stock: bfloat16 [32, 512, 16384], P('real', 'sky'), may hold values from -6 to 6
- plane_pick: int32 [4], replicated, may hold values from 0 to 31, as said below
- col_shift: int32 [16, 4], P('real'), may hold values from 0 to 16383
- mirror: int32 [16, 4], P('real'), may hold values from 0 to 1
- subcell: int32 [64, 16], P('sky'), may hold values from 0 to 15
- lens_weight: float32 [4], replicated, may hold values from 0.02 to 0.08
Outputs:
- deflect: float32 [2, 16, 512, 2048], P(None, 'real', 'sky')
- distort: float32 [4, 16, 512, 2048], P(None, 'real', 'sky')
The draws below stay inside these ranges and needn't reach their ends.
Inputs may be any that keep to these rules, and one draw needn't show every extreme that they name: `plane_pick`: the 4 entries are distinct stored entries; entry q is held by the realization group q // 2.
All inputs are finite; a program needn't handle non-finite values.
Results may differ from the reference program's by a relative error of at most 0.0003.
Values may be sent and summed in bfloat16 or wider, within the bound.
No kernel may reach another device: no remote copies, remote signals or barrier semaphores. Data moves between devices by JAX's collectives and lax.ppermute only.
A program may use at most 64 MiB of HBM per device.

```python
import math
import jax
import jax.numpy as jnp
from jax import lax

COLS = 2048
PLANE_COLS = 16384
PLANES = 4
SUB = 4
TILE_R = 8
TILE_C = 128
WIN_ROWS = 512
STOCK = 32
N_REAL = 16


def draw_plane_pick(key, part):
    first_key = jax.random.fold_in(key, 11)
    second_key = jax.random.fold_in(key, 23)
    middle = jax.random.permutation(first_key, STOCK - 2)[:PLANES - 2] + 1
    chosen = jnp.concatenate([jnp.array([0, STOCK - 1], jnp.int32), middle.astype(jnp.int32)])
    order = jax.random.permutation(second_key, PLANES)
    return chosen[order].astype(jnp.int32)


def touch_ends(values, rng, low, largest):
    shape = values.shape
    place = [jax.random.randint(jax.random.fold_in(rng, axis), (), 0, shape[axis]) for axis in range(len(shape))]
    values = values.at[tuple(place)].set(low)
    longest = shape.index(max(shape))
    place[longest] = (place[longest] + 1) % shape[longest]
    return values.at[tuple(place)].set(largest)


def block_levels(stream_key, shape, split, least, largest):
    gain = 1.0
    for position, blocks in split:
        draws = jax.random.uniform(jax.random.fold_in(jax.random.fold_in(stream_key, 6), position), (blocks,), jnp.float32, least / len(split), largest / len(split))
        gain = gain * jnp.repeat(jnp.exp(draws), shape[position] // blocks).reshape((-1,) + (1,) * (len(shape) - 1 - position))
    return gain


def scatter_about(rng, extent, spread, reach, split=(), held_as=jnp.bfloat16):
    factor_of = block_levels(rng, extent, split, -0.22, 0.18) if split else 1.0
    values = jax.random.normal(rng, extent, jnp.float32) * spread * factor_of
    return jnp.minimum(jnp.maximum(values, -reach), reach).astype(held_as)


def setup_inputs(seed: int = 0) -> dict:
    key_list = jax.random.split(jax.random.key(seed), 7)
    return {
        "potential_stock": scatter_about(key_list[0], (STOCK, WIN_ROWS, PLANE_COLS), 1.0, 6.0, ((0, 16), (1, 16))),
        "plane_pick": draw_plane_pick(jax.random.fold_in(key_list[6], 71), 0),
        "col_shift": touch_ends(jax.random.randint(key_list[2], (N_REAL, PLANES), 0, PLANE_COLS), jax.random.fold_in(key_list[2], 1), 0, PLANE_COLS - 1).astype(jnp.int32),
        "mirror": touch_ends(jax.random.randint(key_list[3], (N_REAL, PLANES), 0, 2), jax.random.fold_in(key_list[3], 1), 0, 1).astype(jnp.int32),
        "subcell": touch_ends(jax.random.randint(key_list[4], (WIN_ROWS // TILE_R, COLS // TILE_C), 0, SUB * SUB), jax.random.fold_in(key_list[4], 1), 0, (SUB * SUB) - 1).astype(jnp.int32),
        "lens_weight": jnp.clip(jnp.exp(jax.random.uniform(key_list[5], (PLANES,), jnp.float32, math.log(0.02), math.log(0.08))), 0.02, 0.08),
    }


first_coef = (1.0 / 12.0, -8.0 / 12.0, 0.0, 8.0 / 12.0, -1.0 / 12.0)
second_coef = (-1.0 / 12.0, 16.0 / 12.0, -30.0 / 12.0, 16.0 / 12.0, -1.0 / 12.0)


def cubic_weights(frac):
    sq = frac * frac
    cube = sq * frac
    return ((-cube + 2.0 * sq - frac) * 0.5, (3.0 * cube - 5.0 * sq + 2.0) * 0.5,
            (-3.0 * cube + 4.0 * sq + frac) * 0.5, (cube - sq) * 0.5)


def tap_weights(subcell):
    frac_x = ((subcell % SUB).astype(jnp.float32) + 0.5) / SUB
    frac_y = ((subcell // SUB).astype(jnp.float32) + 0.5) / SUB
    weights_x = tuple(w[:, None, :, None] for w in cubic_weights(frac_x))
    weights_y = tuple(w[:, None, :, None] for w in cubic_weights(frac_y))
    return weights_x, weights_y


def derivatives(tile):
    nrows = tile.shape[0] - 5
    ncols = tile.shape[1] - 5

    def window(drow, dcol):
        return tile[3 + drow:3 + drow + nrows, 3 + dcol:3 + dcol + ncols]

    grad_x = sum(first_coef[q] * window(0, q - 2) for q in range(5) if q != 2)
    grad_y = sum(first_coef[q] * window(q - 2, 0) for q in range(5) if q != 2)
    hess_xx = sum(second_coef[q] * window(0, q - 2) for q in range(5))
    hess_yy = sum(second_coef[q] * window(q - 2, 0) for q in range(5))
    hess_xy = sum(first_coef[p] * first_coef[q] * window(p - 2, q - 2)
                  for p in range(5) for q in range(5) if p != 2 and q != 2)
    return grad_x, grad_y, hess_xx, hess_yy, hess_xy


def sample(field, weights_x, weights_y, nrows, ncols):
    total = jnp.zeros((nrows // TILE_R, TILE_R, ncols // TILE_C, TILE_C), jnp.float32)
    for brow in range(4):
        inner = jnp.zeros_like(total)
        for acol in range(4):
            piece = field[brow:brow + nrows, acol:acol + ncols]
            piece = piece.reshape(nrows // TILE_R, TILE_R, ncols // TILE_C, TILE_C)
            inner = inner + weights_x[acol] * piece
        total = total + weights_y[brow] * inner
    return total.reshape(nrows, ncols)


def advance(state, tile, weights_x, weights_y, lens):
    nrows = tile.shape[0] - 8
    ncols = tile.shape[1] - 8
    fields = derivatives(tile.astype(jnp.float32))
    grad_x, grad_y, hess_xx, hess_yy, hess_xy = [sample(f, weights_x, weights_y, nrows, ncols) for f in fields]
    shift_x, shift_y, a_11, a_12, a_21, a_22 = state
    shift_x = shift_x + lens * grad_x
    shift_y = shift_y + lens * grad_y
    new_11 = a_11 - lens * (hess_xx * a_11 + hess_xy * a_21)
    new_12 = a_12 - lens * (hess_xx * a_12 + hess_xy * a_22)
    new_21 = a_21 - lens * (hess_xy * a_11 + hess_yy * a_21)
    new_22 = a_22 - lens * (hess_xy * a_12 + hess_yy * a_22)
    return (shift_x, shift_y, new_11, new_12, new_21, new_22)


def reference(potential_stock, plane_pick, col_shift, mirror, subcell, lens_weight):
    weights_x, weights_y = tap_weights(subcell)
    offsets = jnp.arange(-4, COLS + 4, dtype=jnp.int32)

    def trace_one(pair):
        shift_row, mirror_row = pair
        zeros = jnp.zeros((WIN_ROWS, COLS), jnp.float32)
        ones = jnp.ones((WIN_ROWS, COLS), jnp.float32)
        state = (zeros, zeros, ones, zeros, zeros, ones)
        for plane in range(PLANES):
            band = potential_stock[plane_pick[plane]]
            flipped = jnp.where(mirror_row[plane] == 1, band[:, ::-1], band)
            columns = ((shift_row[plane] + offsets) % PLANE_COLS).astype(jnp.int32)
            view = jnp.take(flipped, columns, axis=1)
            view = jnp.concatenate([view[-4:], view, view[:4]], axis=0)
            state = advance(state, view, weights_x, weights_y, lens_weight[plane])
        return state

    result = lax.map(trace_one, (col_shift, mirror))
    deflect = jnp.stack([result[0], result[1]])
    distort = jnp.stack([result[2], result[3], result[4], result[5]])
    return deflect, distort
```

```python
import functools

import jax
import jax.numpy as jnp
import numpy as np
from jax import lax
from jax.experimental import pallas as pl
from jax.experimental.pallas import tpu as pltpu
from jax.sharding import PartitionSpec as P

PLANES = 4
ROWS = 32
TILES = 16
BAND = 16384
WIN = 18 * 128
SCALE = 12288

BF = jnp.bfloat16
F32 = jnp.float32
I32 = jnp.int32


def cubic_ints(n):
    return (
        -(n**3) + 16 * n**2 - 64 * n,
        3 * n**3 - 40 * n**2 + 1024,
        -3 * n**3 + 32 * n**2 + 64 * n,
        n**3 - 8 * n**2,
    )


def filters_1d():
    first = {-2: 1, -1: -8, 1: 8, 2: -1}
    second = {-2: -1, -1: 16, 0: -30, 1: 16, 2: -1}
    out = np.zeros((4, 3, 8), np.int64)
    for f in range(4):
        ints = cubic_ints(2 * f + 1)
        for b, w in zip(range(-1, 3), ints):
            out[f, 0, b + 3] += 12 * w
            for d, v in first.items():
                out[f, 1, b + d + 3] += v * w
            for d, v in second.items():
                out[f, 2, b + d + 3] += v * w
    return out


def x_matrix():
    taps = filters_1d()
    full = np.zeros((256, 12 * 128), np.float64)
    for f in range(4):
        for q in range(3):
            for n in range(8):
                for j in range(128):
                    full[j + 1 + n, (f * 3 + q) * 128 + j] = taps[f, q, n]
    high = full.astype(jnp.bfloat16).astype(np.float64)
    low = full - high
    assert np.array_equal(low.astype(jnp.bfloat16).astype(np.float64), low)
    return np.concatenate([high, low], axis=0).astype(jnp.bfloat16)


def y_table():
    taps = filters_1d().astype(np.float64) / (float(SCALE) * float(SCALE))
    return taps.astype(np.float32).reshape(-1)


def edge_rows():
    s = np.zeros((32, 128), np.float32)
    for p in range(PLANES):
        for q in range(4):
            s[4 * p + q, 32 * p + 28 + q] = 1
            s[16 + 4 * p + q, 32 * p + q] = 1
    return s.astype(jnp.bfloat16)


def halo_rows():
    s = np.zeros((64, 32), np.float32)
    for p in range(PLANES):
        for q in range(4):
            s[16 * p + 4 + q, 4 * p + q] = 1
            s[16 * p + 8 + q, 16 + 4 * p + q] = 1
    return s.astype(jnp.bfloat16)


def slot_planes(pick_ref, chip, slots):
    planes = [jnp.int32(-1)] * slots
    count = jnp.int32(0)
    for p in range(PLANES):
        mine = pick_ref[p] // 4 == chip
        for j in range(slots):
            planes[j] = jnp.where(mine & (count == j), p, planes[j])
        count = count + mine.astype(I32)
    return planes


def cut_kernel(slots, info, pick, t_own, t0, t1, t2, t3, own, mate, out_self, o0, o1, o2, o3, ext, sem_in, sem_out):
    chip, core = info[0], info[1]
    planes = slot_planes(pick, chip, slots)
    tins = (t0, t1, t2, t3)
    outs = (o0, o1, o2, o3)

    def fetch(ref, entry, j):
        return (
            pltpu.make_async_copy(ref.at[entry], ext.at[j, :, pl.ds(0, BAND)], sem_in.at[j, 0]),
            pltpu.make_async_copy(ref.at[entry, :, pl.ds(0, WIN)], ext.at[j, :, pl.ds(BAND, WIN)], sem_in.at[j, 1]),
        )

    for j in range(slots):
        entry = pick[jnp.maximum(planes[j], 0)]
        here = (planes[j] < 0) | ((entry // 2) % 2 == core)

        @pl.when(here)
        def _():
            for copy in fetch(own, entry % 2, j):
                copy.start()

        @pl.when(jnp.logical_not(here))
        def _():
            for copy in fetch(mate, entry % 2, j):
                copy.start()

    copies = []
    for j in range(slots):
        for copy in fetch(own, 0, j):
            copy.wait()
        plane = jnp.maximum(planes[j], 0)

        def cut(tile, dst, s):
            start = pl.multiple_of((tile & 127) * 128, 128)
            copy = pltpu.make_async_copy(ext.at[j, :, pl.ds(start, WIN)], dst, sem_out.at[j, s])
            copy.start()
            copies.append(copy)

        for i in range(4):
            for e in range(2):
                cut(tins[(4 - i) % 4][e * PLANES + plane], outs[i].at[e, j], 2 * i + e)
        cut(t_own[plane], out_self.at[j], 8)
    for copy in copies:
        copy.wait()


def select_kernel(slots, info, pick, s_ref, here, r0, r1, r2, r3, w0, w1, w2, w3, main, edges, sem):
    chip, core = info[0], info[1]
    zhi, y = chip // 4, chip % 4
    recv = (r0, r1, r2, r3)
    swap = (w0, w1, w2, w3)
    ranks = []
    for p in range(PLANES):
        rank = jnp.int32(0)
        for q in range(p):
            rank = rank + (pick[q] // 4 == pick[p] // 4).astype(I32)
        ranks.append(rank if slots > 1 else 0)
    for p in range(PLANES):
        owner = pick[p] // 4
        same = owner == chip
        side = jnp.where(owner // 4 == zhi, 1, 0)
        step = (y - owner % 4 + 4) % 4

        @pl.when(same)
        def _():
            pltpu.make_async_copy(here.at[ranks[p]], main.at[p], sem.at[p]).start()

        for i in range(4):

            @pl.when(jnp.logical_not(same) & (step == i) & (side == core))
            def _():
                pltpu.make_async_copy(recv[i].at[0, ranks[p]], main.at[p], sem.at[p]).start()

            @pl.when(jnp.logical_not(same) & (step == i) & (side != core))
            def _():
                pltpu.make_async_copy(swap[i].at[1, ranks[p]], main.at[p], sem.at[p]).start()

    for p in range(PLANES):
        pltpu.make_async_copy(here.at[0], main.at[p], sem.at[p]).wait()
    rows = main[...].reshape(PLANES * ROWS, WIN)
    edges[...] = jnp.dot(s_ref[...], rows, preferred_element_type=F32).astype(BF)


def ray_kernel(geo, sub, lens, ytab, halo_ref, w_ref, main, up, down, deflect, distort, view, field):
    lane = lax.broadcasted_iota(I32, (16, 128), 1)
    edge = jnp.concatenate([up[...], down[...]], axis=0)

    for k in range(PLANES):
        rest, flip = geo[k], geo[PLANES + k]
        index = jnp.where(flip == 1, rest + 127 - lane, rest + lane)
        low = index < 128
        index = index & 127
        hrow = jnp.dot(halo_ref[pl.ds(16 * k, 16), :], edge, preferred_element_type=F32)

        def moved(b):
            cols = pl.ds(b * 128, 128)
            parts = [main[k, pl.ds(16 * h, 16), cols].astype(F32) for h in range(2)]
            parts.append(hrow[:, b * 128 : b * 128 + 128])
            return [jnp.take_along_axis(x, index, axis=1, mode="promise_in_bounds") for x in parts]

        before = moved(0)
        for b in range(17):
            after = moved(b + 1)
            c = jnp.where(flip == 1, 16 - b, b)
            for h in range(3):
                tile = jnp.where(low, before[h], after[h]).astype(BF)
                view[c + 1, pl.ds(16 * h, 16), pl.ds(0, 128)] = tile
                view[c, pl.ds(16 * h, 16), pl.ds(128, 128)] = tile
            before = after

        group = 4
        for n in range(6):
            for g in range(TILES // group):
                lhs = view[pl.ds(1 + g * group, group)].reshape(48 * group, 256)
                lhs = jnp.concatenate([lhs, lhs], axis=1)
                res = jnp.dot(lhs, w_ref[:, pl.ds(n * 256, 256)], preferred_element_type=F32)
                res = res.reshape(group, 48, 256)
                for half in range(2):
                    fx, q = divmod(2 * n + half, 3)
                    part = res[:, :, half * 128 : half * 128 + 128]
                    cs = pl.ds(g * group, group)
                    field[k, fx, q, cs, pl.ds(8, 32), :] = part[:, :32]
                    field[k, fx, q, cs, pl.ds(0, 8), :] = part[:, 32:40]
                    field[k, fx, q, cs, pl.ds(40, 8), :] = part[:, 40:48]

    for t in range(4):

        def tile(c, carry):
            o = sub[t * TILES + c]
            fx, fy = o % 4, o // 4
            wy = [[ytab[fy * 24 + q * 8 + n] for n in range(8)] for q in range(3)]
            one = jnp.ones((8, 128), F32)
            zero = jnp.zeros((8, 128), F32)
            dx, dy, a11, a12, a21, a22 = zero, zero, one, zero, zero, one
            for k in range(PLANES):

                def taps(q, lo, hi):
                    return {n: field[k, fx, q, c, pl.ds(8 * t + 5 + n, 8), :] for n in range(lo, hi)}

                def filt(vals, q, lo, hi):
                    terms = [wy[q][n] * vals[n] for n in range(lo, hi)]
                    while len(terms) > 1:
                        terms = [a + b for a, b in zip(terms[::2], terms[1::2])] + ([terms[-1]] if len(terms) % 2 else [])
                    return terms[0]

                s = lens[k]
                v1 = taps(1, 0, 8)
                gx = filt(v1, 0, 2, 6)
                hxy = filt(v1, 1, 0, 8) * s
                v0 = taps(0, 0, 8)
                gy = filt(v0, 1, 0, 8)
                hyy = filt(v0, 2, 0, 8) * s
                v2 = taps(2, 2, 6)
                hxx = filt(v2, 0, 2, 6) * s
                dx = dx + s * gx
                dy = dy + s * gy
                b11 = a11 - (hxx * a11 + hxy * a21)
                b12 = a12 - (hxx * a12 + hxy * a22)
                b21 = a21 - (hxy * a11 + hyy * a21)
                b22 = a22 - (hxy * a12 + hyy * a22)
                a11, a12, a21, a22 = b11, b12, b21, b22
            cols = pl.ds(pl.multiple_of(c * 128, 128), 128)
            rows = pl.ds(8 * t, 8)
            deflect[0, 0, rows, cols] = dx
            deflect[1, 0, rows, cols] = dy
            distort[0, 0, rows, cols] = a11
            distort[1, 0, rows, cols] = a12
            distort[2, 0, rows, cols] = a21
            distort[3, 0, rows, cols] = a22
            return carry

        lax.fori_loop(0, TILES, tile, 0)


SMEM = pl.BlockSpec(memory_space=pltpu.SMEM)
VMEM = pl.BlockSpec(memory_space=pltpu.VMEM)
ANY = pl.BlockSpec(memory_space=pl.ANY)


def real_index(zhi, y, core):
    return (zhi * 4 + y) * 2 + core


def core_pairs():
    return [(r, r ^ 1) for r in range(16)]


def step_pairs(i):
    pairs = []
    for zhi in range(2):
        for y in range(4):
            pairs.append((real_index(zhi, y, 0), real_index(1 - zhi, (y + i) % 4, 0)))
            if i:
                pairs.append((real_index(zhi, y, 1), real_index(zhi, (y + i) % 4, 1)))
    return pairs


def cut(slots, info, pick, t_own, tins, own, mate):
    win = jax.ShapeDtypeStruct((2, slots, ROWS, WIN), BF)
    return pl.pallas_call(
        functools.partial(cut_kernel, slots),
        out_shape=[jax.ShapeDtypeStruct((slots, ROWS, WIN), BF)] + [win] * 4,
        in_specs=[SMEM] * 7 + [ANY] * 2,
        out_specs=[ANY] * 5,
        scratch_shapes=[
            pltpu.VMEM((slots, ROWS, BAND + WIN), BF),
            pltpu.SemaphoreType.DMA((slots, 2)),
            pltpu.SemaphoreType.DMA((slots, 9)),
        ],
        compiler_params=pltpu.CompilerParams(vmem_limit_bytes=16 * 2**20),
    )(info, pick, t_own, *tins, own, mate)


def select(slots, info, pick, here, recv, swap):
    return pl.pallas_call(
        functools.partial(select_kernel, slots),
        out_shape=[
            jax.ShapeDtypeStruct((PLANES, ROWS, WIN), BF),
            jax.ShapeDtypeStruct((32, WIN), BF),
        ],
        in_specs=[SMEM] * 2 + [VMEM] + [ANY] * 9,
        out_specs=[VMEM] * 2,
        scratch_shapes=[pltpu.SemaphoreType.DMA((PLANES,))],
        compiler_params=pltpu.CompilerParams(vmem_limit_bytes=16 * 2**20),
    )(info, pick, jnp.asarray(edge_rows()), here, *recv, *swap)


def rays(geo, sub, lens, main, up, down):
    return pl.pallas_call(
        ray_kernel,
        out_shape=[
            jax.ShapeDtypeStruct((2, 1, ROWS, TILES * 128), F32),
            jax.ShapeDtypeStruct((4, 1, ROWS, TILES * 128), F32),
        ],
        in_specs=[SMEM] * 4 + [VMEM] * 5,
        out_specs=[VMEM] * 2,
        scratch_shapes=[
            pltpu.VMEM((18, 48, 256), BF),
            pltpu.VMEM((PLANES, 4, 3, TILES, 48, 128), F32),
        ],
        compiler_params=pltpu.CompilerParams(vmem_limit_bytes=48 * 2**20),
    )(geo, sub, lens, jnp.asarray(y_table()), jnp.asarray(halo_rows()), jnp.asarray(x_matrix()), main, up, down)


def exchange(slots, info, pick, t_own, tins, own, mate):
    here, *outs = cut(slots, info, pick, t_own, tins, own, mate)
    recv = [lax.ppermute(x, "real", step_pairs(i)) for i, x in enumerate(outs)]
    swap = [lax.ppermute(x, "real", core_pairs()) for x in recv]
    return tuple(select(slots, info, pick, here, recv, swap))


def body(potential_stock, plane_pick, col_shift, mirror, subcell, lens_weight):
    me = lax.axis_index("real")
    info = jnp.stack([me // 2, me % 2]).astype(I32)
    shift, flip = col_shift[0], mirror[0]
    start = jnp.where(flip == 1, BAND - 4 - 2168 - shift, shift - 4) & (BAND - 1)
    first, rest = start // 128, start % 128

    mate = lax.ppermute(potential_stock, "real", core_pairs())
    first_mate = lax.ppermute(first, "real", core_pairs())
    pair = jnp.concatenate([first, first_mate])
    tins = [lax.ppermute(pair, "real", step_pairs(i)) for i in range(4)]

    chips = plane_pick // 4
    most = jnp.max(jnp.sum((chips[:, None] == chips[None, :]).astype(I32), axis=1))
    branch = jnp.where(most <= 1, 0, jnp.where(most <= 2, 1, 2)).astype(I32)
    main, edges = lax.switch(
        branch,
        [functools.partial(exchange, k) for k in (1, 2, 4)],
        info, plane_pick, first, tins, potential_stock, mate,
    )
    n = lax.axis_size("sky")
    up = lax.ppermute(edges[:16], "sky", [(i, (i + 1) % n) for i in range(n)])
    down = lax.ppermute(edges[16:], "sky", [((i + 1) % n, i) for i in range(n)])
    geo = jnp.concatenate([rest, flip])
    return tuple(rays(geo, subcell.reshape(-1), lens_weight, main, up, down))


def solution(mesh):
    return jax.shard_map(
        body,
        mesh=mesh,
        in_specs=(
            P("real", "sky", None),
            P(),
            P("real", None),
            P("real", None),
            P("sky", None),
            P(),
        ),
        out_specs=(P(None, "real", "sky", None), P(None, "real", "sky", None)),
        check_vma=False,
    )
```

```python
import functools

import jax
import jax.numpy as jnp
import numpy as np
from jax import lax
from jax.experimental import pallas as pl
from jax.experimental.pallas import tpu as pltpu
from jax.sharding import PartitionSpec as P

PLANES = 4
ROWS = 32
HALF = 16
TILES = 16
BAND = 16384
WIN = 18 * 128
SCALE = 12288

BF = jnp.bfloat16
F32 = jnp.float32
I32 = jnp.int32


def cubic_ints(n):
    return (
        -(n**3) + 16 * n**2 - 64 * n,
        3 * n**3 - 40 * n**2 + 1024,
        -3 * n**3 + 32 * n**2 + 64 * n,
        n**3 - 8 * n**2,
    )


def filters_1d():
    first = {-2: 1, -1: -8, 1: 8, 2: -1}
    second = {-2: -1, -1: 16, 0: -30, 1: 16, 2: -1}
    out = np.zeros((4, 3, 8), np.int64)
    for f in range(4):
        ints = cubic_ints(2 * f + 1)
        for b, w in zip(range(-1, 3), ints):
            out[f, 0, b + 3] += 12 * w
            for d, v in first.items():
                out[f, 1, b + d + 3] += v * w
            for d, v in second.items():
                out[f, 2, b + d + 3] += v * w
    return out


def x_matrix():
    taps = filters_1d()
    full = np.zeros((256, 12 * 128), np.float64)
    for f in range(4):
        for q in range(3):
            for n in range(8):
                for j in range(128):
                    full[j + 1 + n, (f * 3 + q) * 128 + j] = taps[f, q, n]
    high = full.astype(jnp.bfloat16).astype(np.float64)
    low = full - high
    assert np.array_equal(low.astype(jnp.bfloat16).astype(np.float64), low)
    return np.concatenate([high, low], axis=0).astype(jnp.bfloat16)


def y_table():
    taps = filters_1d().astype(np.float64) / (float(SCALE) * float(SCALE))
    return taps.astype(np.float32).reshape(-1)


def edge_rows():
    s = np.zeros((2, 32, 128), np.float32)
    for c in range(2):
        for part in range(2 * PLANES):
            for q in range(4):
                s[c, 4 * part + q, 16 * part + 12 * c + q] = 1
    return s.astype(jnp.bfloat16)


def halo_rows():
    s = np.zeros((2, 64, 64), np.float32)
    for p in range(PLANES):
        for q in range(4):
            for c in range(2):
                received, swapped = 4 * p + q, 48 + 4 * p + q
                above, below = (swapped, received) if c == 0 else (received, swapped)
                s[c, 16 * p + 4 + q, above] = 1
                s[c, 16 * p + 8 + q, below] = 1
    return s.astype(jnp.bfloat16)


def slot_planes(pick_ref, chip, slots):
    planes = [jnp.int32(-1)] * slots
    count = jnp.int32(0)
    for p in range(PLANES):
        mine = pick_ref[p] // 4 == chip
        for j in range(slots):
            planes[j] = jnp.where(mine & (count == j), p, planes[j])
        count = count + mine.astype(I32)
    return planes


def half_kernel(slots, info, pick, own, mate, out, sem):
    chip, core = info[0], info[1]
    planes = slot_planes(pick, chip, slots)
    rows = pl.ds(pl.multiple_of(core * HALF, HALF), HALF)
    for j in range(slots):
        entry = pick[jnp.maximum(planes[j], 0)]
        here = (planes[j] < 0) | ((entry // 2) % 2 == core)

        @pl.when(here)
        def _():
            pltpu.make_async_copy(own.at[entry % 2, rows], out.at[j], sem.at[j]).start()

        @pl.when(jnp.logical_not(here))
        def _():
            pltpu.make_async_copy(mate.at[entry % 2, rows], out.at[j], sem.at[j]).start()

    for j in range(slots):
        pltpu.make_async_copy(own.at[0, rows], out.at[j], sem.at[j]).wait()


def cut_kernel(slots, far, info, pick, t0, t1, t2, t3, band, o0, o1, o2, o3, ext, sem_in, sem_out):
    chip = (info[0] + 4 * far) % 8
    planes = slot_planes(pick, chip, slots)
    tins = (t0, t1, t2, t3)
    outs = (o0, o1, o2, o3)
    fetches = []
    for j in range(slots):
        fetches.append((
            pltpu.make_async_copy(band.at[j], ext.at[j, :, pl.ds(0, BAND)], sem_in.at[j, 0]),
            pltpu.make_async_copy(band.at[j, :, pl.ds(0, WIN)], ext.at[j, :, pl.ds(BAND, WIN)], sem_in.at[j, 1]),
        ))
        for copy in fetches[j]:
            copy.start()
    copies = []
    for j in range(slots):
        for copy in fetches[j]:
            copy.wait()
        plane = jnp.maximum(planes[j], 0)
        for i in range(4):
            for e in range(2):
                tile = tins[(4 - i) % 4][e * PLANES + plane] & 127
                start = pl.multiple_of(tile * 128, 128)
                copy = pltpu.make_async_copy(
                    ext.at[j, :, pl.ds(start, WIN)], outs[i].at[e, j], sem_out.at[j, 2 * i + e]
                )
                copy.start()
                copies.append(copy)
    for copy in copies:
        copy.wait()


def select_kernel(slots, info, pick, s_ref, *refs):
    near, far = refs[:4], refs[4:8]
    parts, edges, sem = refs[8:]
    chip, core = info[0], info[1]
    zhi, y = chip // 4, chip % 4
    for p in range(PLANES):
        rank = jnp.int32(0)
        for q in range(p):
            rank = rank + (pick[q] // 4 == pick[p] // 4).astype(I32)
        rank = rank if slots > 1 else 0
        owner = pick[p] // 4
        step = (y - owner % 4 + 4) % 4
        same = owner // 4 == zhi
        for i in range(4):
            for group, here in ((near, same), (far, jnp.logical_not(same))):

                @pl.when(here & (step == i))
                def _():
                    for e in range(2):
                        pltpu.make_async_copy(group[i].at[e, rank], parts.at[e, p], sem.at[e, p]).start()

    for p in range(PLANES):
        for e in range(2):
            pltpu.make_async_copy(near[0].at[0, 0], parts.at[e, p], sem.at[e, p]).wait()
    rows = parts[...].reshape(2 * PLANES * HALF, WIN)
    edges[...] = jnp.dot(s_ref[core], rows, preferred_element_type=F32).astype(BF)


def ray_kernel(geo, sub, lens, ytab, halo_ref, w_ref, mine, swapped, got, got_swapped, deflect, distort, view, field):
    lane = lax.broadcasted_iota(I32, (16, 128), 1)
    core = geo[2 * PLANES]
    edge = jnp.concatenate([got[...], got_swapped[...]], axis=0)

    for k in range(PLANES):
        rest, flip = geo[k], geo[PLANES + k]
        index = jnp.where(flip == 1, rest + 127 - lane, rest + lane)
        low = index < 128
        index = index & 127
        hrow = jnp.dot(halo_ref[core, pl.ds(16 * k, 16), :], edge, preferred_element_type=F32)

        def moved(b):
            cols = pl.ds(b * 128, 128)
            m, w = mine[0, k, :, cols], swapped[1, k, :, cols]
            parts = [jnp.where(core == 0, m, w).astype(F32), jnp.where(core == 0, w, m).astype(F32)]
            parts.append(hrow[:, b * 128 : b * 128 + 128])
            return [jnp.take_along_axis(x, index, axis=1, mode="promise_in_bounds") for x in parts]

        before = moved(0)
        for b in range(17):
            after = moved(b + 1)
            c = jnp.where(flip == 1, 16 - b, b)
            for h in range(3):
                tile = jnp.where(low, before[h], after[h]).astype(BF)
                view[c + 1, pl.ds(16 * h, 16), pl.ds(0, 128)] = tile
                view[c, pl.ds(16 * h, 16), pl.ds(128, 128)] = tile
            before = after

        group = 4
        for n in range(6):
            for g in range(TILES // group):
                lhs = view[pl.ds(1 + g * group, group)].reshape(48 * group, 256)
                lhs = jnp.concatenate([lhs, lhs], axis=1)
                res = jnp.dot(lhs, w_ref[:, pl.ds(n * 256, 256)], preferred_element_type=F32)
                res = res.reshape(group, 48, 256)
                for half in range(2):
                    fx, q = divmod(2 * n + half, 3)
                    part = res[:, :, half * 128 : half * 128 + 128]
                    cs = pl.ds(g * group, group)
                    field[k, fx, q, cs, pl.ds(8, 32), :] = part[:, :32]
                    field[k, fx, q, cs, pl.ds(0, 8), :] = part[:, 32:40]
                    field[k, fx, q, cs, pl.ds(40, 8), :] = part[:, 40:48]

    for t in range(4):

        def tile(c, carry):
            o = sub[t * TILES + c]
            fx, fy = o % 4, o // 4
            wy = [[ytab[fy * 24 + q * 8 + n] for n in range(8)] for q in range(3)]
            one = jnp.ones((8, 128), F32)
            zero = jnp.zeros((8, 128), F32)
            dx, dy, a11, a12, a21, a22 = zero, zero, one, zero, zero, one
            for k in range(PLANES):

                def taps(q, lo, hi):
                    return {n: field[k, fx, q, c, pl.ds(8 * t + 5 + n, 8), :] for n in range(lo, hi)}

                def filt(vals, q, lo, hi):
                    terms = [wy[q][n] * vals[n] for n in range(lo, hi)]
                    while len(terms) > 1:
                        terms = [a + b for a, b in zip(terms[::2], terms[1::2])] + ([terms[-1]] if len(terms) % 2 else [])
                    return terms[0]

                s = lens[k]
                v1 = taps(1, 0, 8)
                gx = filt(v1, 0, 2, 6)
                hxy = filt(v1, 1, 0, 8) * s
                v0 = taps(0, 0, 8)
                gy = filt(v0, 1, 0, 8)
                hyy = filt(v0, 2, 0, 8) * s
                v2 = taps(2, 2, 6)
                hxx = filt(v2, 0, 2, 6) * s
                dx = dx + s * gx
                dy = dy + s * gy
                b11 = a11 - (hxx * a11 + hxy * a21)
                b12 = a12 - (hxx * a12 + hxy * a22)
                b21 = a21 - (hxy * a11 + hyy * a21)
                b22 = a22 - (hxy * a12 + hyy * a22)
                a11, a12, a21, a22 = b11, b12, b21, b22
            cols = pl.ds(pl.multiple_of(c * 128, 128), 128)
            rows = pl.ds(8 * t, 8)
            deflect[0, 0, rows, cols] = dx
            deflect[1, 0, rows, cols] = dy
            distort[0, 0, rows, cols] = a11
            distort[1, 0, rows, cols] = a12
            distort[2, 0, rows, cols] = a21
            distort[3, 0, rows, cols] = a22
            return carry

        lax.fori_loop(0, TILES, tile, 0)


SMEM = pl.BlockSpec(memory_space=pltpu.SMEM)
VMEM = pl.BlockSpec(memory_space=pltpu.VMEM)
ANY = pl.BlockSpec(memory_space=pl.ANY)


def real_index(zhi, y, core):
    return (zhi * 4 + y) * 2 + core


def core_pairs():
    return [(r, r ^ 1) for r in range(16)]


def y_pairs(i):
    return [
        (real_index(zhi, y, c), real_index(zhi, (y + i) % 4, c)) for zhi in range(2) for y in range(4) for c in range(2)
    ]


def z_pairs():
    return [(r, (r + 8) % 16) for r in range(16)]


def edge_pairs(n):
    return [(r * n + s, r * n + (s + (1 if r % 2 else n - 1)) % n) for r in range(16) for s in range(n)]


def params(mib):
    return pltpu.CompilerParams(vmem_limit_bytes=mib * 2**20)


def halves(slots, info, pick, own, mate):
    return pl.pallas_call(
        functools.partial(half_kernel, slots),
        out_shape=jax.ShapeDtypeStruct((slots, HALF, BAND), BF),
        in_specs=[SMEM] * 2 + [ANY] * 2,
        out_specs=ANY,
        scratch_shapes=[pltpu.SemaphoreType.DMA((slots,))],
        compiler_params=params(16),
    )(info, pick, own, mate)


def cut(slots, far, info, pick, tins, band):
    win = jax.ShapeDtypeStruct((2, slots, HALF, WIN), BF)
    return pl.pallas_call(
        functools.partial(cut_kernel, slots, far),
        out_shape=[win] * 4,
        in_specs=[SMEM] * 6 + [ANY],
        out_specs=[ANY] * 4,
        scratch_shapes=[
            pltpu.VMEM((slots, HALF, BAND + WIN), BF),
            pltpu.SemaphoreType.DMA((slots, 2)),
            pltpu.SemaphoreType.DMA((slots, 8)),
        ],
        compiler_params=params(16),
    )(info, pick, *tins, band)


def select(slots, info, pick, near, far):
    return pl.pallas_call(
        functools.partial(select_kernel, slots),
        out_shape=[
            jax.ShapeDtypeStruct((2, PLANES, HALF, WIN), BF),
            jax.ShapeDtypeStruct((32, WIN), BF),
        ],
        in_specs=[SMEM] * 2 + [VMEM] + [ANY] * 8,
        out_specs=[VMEM] * 2,
        scratch_shapes=[pltpu.SemaphoreType.DMA((2, PLANES))],
        compiler_params=params(16),
    )(info, pick, jnp.asarray(edge_rows()), *near, *far)


def rays(geo, sub, lens, mine, swapped, got, got_swapped):
    return pl.pallas_call(
        ray_kernel,
        out_shape=[
            jax.ShapeDtypeStruct((2, 1, ROWS, TILES * 128), F32),
            jax.ShapeDtypeStruct((4, 1, ROWS, TILES * 128), F32),
        ],
        in_specs=[SMEM] * 4 + [VMEM] * 6,
        out_specs=[VMEM] * 2,
        scratch_shapes=[
            pltpu.VMEM((18, 48, 256), BF),
            pltpu.VMEM((PLANES, 4, 3, TILES, 48, 128), F32),
        ],
        compiler_params=params(48),
    )(
        geo, sub, lens, jnp.asarray(y_table()), jnp.asarray(halo_rows()), jnp.asarray(x_matrix()),
        mine, swapped, got, got_swapped,
    )


def round_y(outs):
    return [outs[0]] + [lax.ppermute(outs[i], "real", y_pairs(i)) for i in range(1, 4)]


def exchange(slots, info, pick, tins, own, mate):
    half = halves(slots, info, pick, own, mate)
    other = lax.ppermute(half, "real", z_pairs())
    near = round_y(cut(slots, 0, info, pick, tins, half))
    far = round_y(cut(slots, 1, info, pick, tins, other))
    return tuple(select(slots, info, pick, near, far))


def body(potential_stock, plane_pick, col_shift, mirror, subcell, lens_weight):
    me = lax.axis_index("real")
    info = jnp.stack([me // 2, me % 2]).astype(I32)
    shift, flip = col_shift[0], mirror[0]
    start = jnp.where(flip == 1, BAND - 4 - 2168 - shift, shift - 4) & (BAND - 1)
    first, rest = start // 128, start % 128

    mate = lax.ppermute(potential_stock, "real", core_pairs())
    pair = jnp.concatenate([first, lax.ppermute(first, "real", core_pairs())])
    tins = [pair] + [lax.ppermute(pair, "real", y_pairs(i)) for i in range(1, 4)]

    chips = plane_pick // 4
    most = jnp.max(jnp.sum((chips[:, None] == chips[None, :]).astype(I32), axis=1))
    branch = jnp.where(most <= 1, 0, jnp.where(most <= 2, 1, 2)).astype(I32)
    parts, edges = lax.switch(
        branch,
        [functools.partial(exchange, k) for k in (1, 2, 4)],
        info, plane_pick, tins, potential_stock, mate,
    )
    got = lax.ppermute(edges, ("real", "sky"), edge_pairs(lax.axis_size("sky")))
    swapped = lax.ppermute(parts, "real", core_pairs())
    got_swapped = lax.ppermute(got, "real", core_pairs())
    geo = jnp.concatenate([rest, flip, info[1:]])
    return tuple(rays(geo, subcell.reshape(-1), lens_weight, parts, swapped, got, got_swapped))


def solution(mesh):
    return jax.shard_map(
        body,
        mesh=mesh,
        in_specs=(
            P("real", "sky", None),
            P(),
            P("real", None),
            P("real", None),
            P("sky", None),
            P(),
        ),
        out_specs=(P(None, "real", "sky", None), P(None, "real", "sky", None)),
        check_vma=False,
    )
```

```python
import functools

import jax
import jax.numpy as jnp
import numpy as np
from jax import lax
from jax.experimental import pallas as pl
from jax.experimental.pallas import tpu as pltpu
from jax.sharding import PartitionSpec as P

PLANES = 4
ROWS = 32
HALF = 16
TILES = 16
BAND = 16384
WIN = 18 * 128
SCALE = 12288

BF = jnp.bfloat16
F32 = jnp.float32
I32 = jnp.int32


def cubic_ints(n):
    return (
        -(n**3) + 16 * n**2 - 64 * n,
        3 * n**3 - 40 * n**2 + 1024,
        -3 * n**3 + 32 * n**2 + 64 * n,
        n**3 - 8 * n**2,
    )


def filters_1d():
    first = {-2: 1, -1: -8, 1: 8, 2: -1}
    second = {-2: -1, -1: 16, 0: -30, 1: 16, 2: -1}
    out = np.zeros((4, 3, 8), np.int64)
    for f in range(4):
        ints = cubic_ints(2 * f + 1)
        for b, w in zip(range(-1, 3), ints):
            out[f, 0, b + 3] += 12 * w
            for d, v in first.items():
                out[f, 1, b + d + 3] += v * w
            for d, v in second.items():
                out[f, 2, b + d + 3] += v * w
    return out


def x_matrix():
    taps = filters_1d()
    full = np.zeros((256, 12 * 128), np.float64)
    for f in range(4):
        for q in range(3):
            for n in range(8):
                for j in range(128):
                    full[j + 1 + n, (f * 3 + q) * 128 + j] = taps[f, q, n]
    high = full.astype(jnp.bfloat16).astype(np.float64)
    low = full - high
    assert np.array_equal(low.astype(jnp.bfloat16).astype(np.float64), low)
    return np.concatenate([high, low], axis=0).astype(jnp.bfloat16)


def y_table():
    taps = filters_1d().astype(np.float64) / (float(SCALE) * float(SCALE))
    return taps.astype(np.float32).reshape(-1)


def edge_rows():
    s = np.zeros((2, 32, 128), np.float32)
    for c in range(2):
        for part in range(2 * PLANES):
            for q in range(4):
                s[c, 4 * part + q, 16 * part + 12 * c + q] = 1
    return s.astype(jnp.bfloat16)


def halo_rows():
    s = np.zeros((2, 64, 64), np.float32)
    for p in range(PLANES):
        for q in range(4):
            for c in range(2):
                received, swapped = 4 * p + q, 48 + 4 * p + q
                above, below = (swapped, received) if c == 0 else (received, swapped)
                s[c, 16 * p + 4 + q, above] = 1
                s[c, 16 * p + 8 + q, below] = 1
    return s.astype(jnp.bfloat16)


def slot_planes(pick_ref, chip, slots):
    planes = [jnp.int32(-1)] * slots
    count = jnp.int32(0)
    for p in range(PLANES):
        mine = pick_ref[p] // 4 == chip
        for j in range(slots):
            planes[j] = jnp.where(mine & (count == j), p, planes[j])
        count = count + mine.astype(I32)
    return planes


def half_kernel(slots, info, pick, own, mate, out, sem):
    chip, core = info[0], info[1]
    planes = slot_planes(pick, chip, slots)
    rows = pl.ds(pl.multiple_of(core * HALF, HALF), HALF)
    for j in range(slots):
        entry = pick[jnp.maximum(planes[j], 0)]
        here = (planes[j] < 0) | ((entry // 2) % 2 == core)

        @pl.when(here)
        def _():
            pltpu.make_async_copy(own.at[entry % 2, rows], out.at[j], sem.at[j]).start()

        @pl.when(jnp.logical_not(here))
        def _():
            pltpu.make_async_copy(mate.at[entry % 2, rows], out.at[j], sem.at[j]).start()

    for j in range(slots):
        pltpu.make_async_copy(own.at[0, rows], out.at[j], sem.at[j]).wait()


def cut_kernel(slots, far, info, pick, t0, t1, t2, t3, band, o0, o1, o2, o3, ext, sem_in, sem_out):
    chip = (info[0] + 4 * far) % 8
    planes = slot_planes(pick, chip, slots)
    tins = (t0, t1, t2, t3)
    outs = (o0, o1, o2, o3)
    fetches = []
    for j in range(slots):
        fetches.append((
            pltpu.make_async_copy(band.at[j], ext.at[j, :, pl.ds(0, BAND)], sem_in.at[j, 0]),
            pltpu.make_async_copy(band.at[j, :, pl.ds(0, WIN)], ext.at[j, :, pl.ds(BAND, WIN)], sem_in.at[j, 1]),
        ))
        for copy in fetches[j]:
            copy.start()
    copies = []
    for j in range(slots):
        for copy in fetches[j]:
            copy.wait()
        plane = jnp.maximum(planes[j], 0)
        for i in range(4):
            for e in range(2):
                tile = tins[(4 - i) % 4][e * PLANES + plane] & 127
                start = pl.multiple_of(tile * 128, 128)
                copy = pltpu.make_async_copy(
                    ext.at[j, :, pl.ds(start, WIN)], outs[i].at[e, j], sem_out.at[j, 2 * i + e]
                )
                copy.start()
                copies.append(copy)
    for copy in copies:
        copy.wait()


def select_kernel(slots, far, info, pick, s_ref, g0, g1, g2, g3, parts, edges, sem):
    chip, core = info[0], info[1]
    zhi, y = chip // 4, chip % 4
    group = (g0, g1, g2, g3)
    for p in range(PLANES):
        rank = jnp.int32(0)
        for q in range(p):
            rank = rank + (pick[q] // 4 == pick[p] // 4).astype(I32)
        rank = rank if slots > 1 else 0
        owner = pick[p] // 4
        step = (y - owner % 4 + 4) % 4
        here = (owner // 4 + zhi) % 2 == far
        for i in range(4):

            @pl.when(here & (step == i))
            def _():
                for e in range(2):
                    pltpu.make_async_copy(group[i].at[e, rank], parts.at[e, p], sem.at[e, p]).start()

        @pl.when(jnp.logical_not(here))
        def _():
            parts[:, p] = jnp.zeros((2, HALF, WIN), BF)

    for p in range(PLANES):

        @pl.when((pick[p] // 16 + zhi) % 2 == far)
        def _():
            for e in range(2):
                pltpu.make_async_copy(g0.at[0, 0], parts.at[e, p], sem.at[e, p]).wait()

    rows = parts[...].reshape(2 * PLANES * HALF, WIN)
    edges[...] = jnp.dot(s_ref[core], rows, preferred_element_type=F32).astype(BF)


def sample_plane(k, tiles, halo, info, geo, sub, lens, ytab, w_ref, mine, swapped, halo_ref, edge, view, field, fields):
    nrow = 48 if halo else 32
    core = info[1]
    rest, flip = geo[k], geo[PLANES + k]
    lane = lax.broadcasted_iota(I32, (16, 128), 1)
    index = jnp.where(flip == 1, rest + 127 - lane, rest + lane)
    low = index < 128
    index = index & 127
    if halo:
        hrow = jnp.dot(
            halo_ref[core, pl.ds(pl.multiple_of(16 * k, 16), 16), :], edge, preferred_element_type=F32
        )

    def moved(b):
        cols = pl.ds(b * 128, 128)
        m, w = mine[0, k, :, cols], swapped[1, k, :, cols]
        parts = [jnp.where(core == 0, m, w).astype(F32), jnp.where(core == 0, w, m).astype(F32)]
        if halo:
            parts.append(hrow[:, b * 128 : b * 128 + 128])
        return [jnp.take_along_axis(x, index, axis=1, mode="promise_in_bounds") for x in parts]

    before = moved(0)
    for b in range(17):
        after = moved(b + 1)
        c = jnp.where(flip == 1, 16 - b, b)
        for h in range(nrow // 16):
            tile = jnp.where(low, before[h], after[h]).astype(BF)
            view[c + 1, pl.ds(16 * h, 16), pl.ds(0, 128)] = tile
            view[c, pl.ds(16 * h, 16), pl.ds(128, 128)] = tile
        before = after

    group = 8
    for n in range(6):
        for g in range(TILES // group):
            lhs = view[pl.ds(1 + g * group, group), pl.ds(0, nrow), :].reshape(nrow * group, 256)
            lhs = jnp.concatenate([lhs, lhs], axis=1)
            res = jnp.dot(lhs, w_ref[:, pl.ds(n * 256, 256)], preferred_element_type=F32)
            res = res.reshape(group, nrow, 256)
            for half in range(2):
                fx, q = divmod(2 * n + half, 3)
                part = res[:, :, half * 128 : half * 128 + 128]
                cs = pl.ds(g * group, group)
                field[fx, q, cs, pl.ds(8, 32), :] = part[:, :32]
                if halo:
                    field[fx, q, cs, pl.ds(0, 8), :] = part[:, 32:40]
                    field[fx, q, cs, pl.ds(40, 8), :] = part[:, 40:48]

    s = lens[k]
    for place, t in enumerate(tiles):

        def tile(c, carry):
            o = sub[t * TILES + c]
            fx, fy = o % 4, o // 4
            wy = [[ytab[fy * 24 + q * 8 + n] * s for n in range(8)] for q in range(3)]

            def taps(q, lo, hi):
                return {n: field[fx, q, c, pl.ds(8 * t + 5 + n, 8), :] for n in range(lo, hi)}

            def filt(vals, q, lo, hi):
                terms = [wy[q][n] * vals[n] for n in range(lo, hi)]
                while len(terms) > 1:
                    odd = [terms[-1]] if len(terms) % 2 else []
                    terms = [a + b for a, b in zip(terms[::2], terms[1::2])] + odd
                return terms[0]

            rows, cols = pl.ds(8 * place, 8), pl.ds(pl.multiple_of(c * 128, 128), 128)
            v1 = taps(1, 0, 8)
            fields[k, 0, rows, cols] = filt(v1, 0, 2, 6)
            fields[k, 4, rows, cols] = filt(v1, 1, 0, 8)
            v0 = taps(0, 0, 8)
            fields[k, 1, rows, cols] = filt(v0, 1, 0, 8)
            fields[k, 3, rows, cols] = filt(v0, 2, 0, 8)
            v2 = taps(2, 2, 6)
            fields[k, 2, rows, cols] = filt(v2, 0, 2, 6)
            return carry

        lax.fori_loop(0, TILES, tile, 0)


def held(info, pick, k):
    return (pick[k] // 16) == (info[0] // 4)


def near_kernel(
    info, pick, geo, sub, lens, ytab, halo_ref, mine, swapped, got, got_swapped, w_hbm, out, w_ref, view, field, fields, sem
):
    weights = pltpu.make_async_copy(w_hbm, w_ref, sem.at[PLANES])
    weights.start()
    edge = jnp.concatenate([got[...], got_swapped[...]], axis=0)
    weights.wait()

    def plane(k, carry):
        @pl.when(held(info, pick, k))
        def _():
            sample_plane(
                k, range(4), True, info, geo, sub, lens, ytab, w_ref, mine, swapped, halo_ref, edge, view, field, fields
            )
            pltpu.make_async_copy(fields.at[k], out.at[k], sem.at[k]).start()

        return carry

    lax.fori_loop(0, PLANES, plane, 0)
    for k in range(PLANES):

        @pl.when(held(info, pick, k))
        def _():
            pltpu.make_async_copy(fields.at[k], out.at[k], sem.at[k]).wait()


def far_kernel(tiles, halo, info, pick, geo, sub, lens, ytab, mine, swapped, w_hbm, near, *refs):
    if halo:
        halo_ref, got, got_swapped, _, _, *refs = refs
        edge = jnp.concatenate([got[...], got_swapped[...]], axis=0)
    else:
        halo_ref = edge = None
    deflect, distort, w_ref, view, field, fields, deflect_v, distort_v, sem, sem_out = refs
    weights = pltpu.make_async_copy(w_hbm, w_ref, sem.at[PLANES, 0])
    weights.start()

    def brought(k):
        return [
            pltpu.make_async_copy(near.at[k, :, pl.ds(8 * t, 8)], fields.at[k, :, pl.ds(8 * i, 8)], sem.at[k, i])
            for i, t in enumerate(tiles)
        ]

    for k in range(PLANES):

        @pl.when(held(info, pick, k))
        def _():
            for copy in brought(k):
                copy.start()

    weights.wait()

    def plane(k, carry):
        @pl.when(jnp.logical_not(held(info, pick, k)))
        def _():
            sample_plane(
                k, tiles, halo, info, geo, sub, lens, ytab, w_ref, mine, swapped, halo_ref, edge, view, field, fields
            )

        return carry

    lax.fori_loop(0, PLANES, plane, 0)
    for k in range(PLANES):

        @pl.when(held(info, pick, k))
        def _():
            for copy in brought(k):
                copy.wait()

    copies = []
    for i, t in enumerate(tiles):
        rows = pl.ds(8 * i, 8)

        def tile(c, carry):
            cols = pl.ds(pl.multiple_of(c * 128, 128), 128)
            one = jnp.ones((8, 128), F32)
            zero = jnp.zeros((8, 128), F32)
            dx, dy, a11, a12, a21, a22 = zero, zero, one, zero, zero, one
            for k in range(PLANES):
                gx, gy, hxx, hyy, hxy = [fields[k, f, rows, cols] for f in range(5)]
                dx = dx + gx
                dy = dy + gy
                b11 = a11 - (hxx * a11 + hxy * a21)
                b12 = a12 - (hxx * a12 + hxy * a22)
                b21 = a21 - (hxy * a11 + hyy * a21)
                b22 = a22 - (hxy * a12 + hyy * a22)
                a11, a12, a21, a22 = b11, b12, b21, b22
            deflect_v[0, 0, rows, cols] = dx
            deflect_v[1, 0, rows, cols] = dy
            distort_v[0, 0, rows, cols] = a11
            distort_v[1, 0, rows, cols] = a12
            distort_v[2, 0, rows, cols] = a21
            distort_v[3, 0, rows, cols] = a22
            return carry

        lax.fori_loop(0, TILES, tile, 0)
        there = pl.ds(8 * t, 8)
        for j, (src, dst) in enumerate(((deflect_v, deflect), (distort_v, distort))):
            copy = pltpu.make_async_copy(src.at[:, :, rows], dst.at[:, :, there], sem_out.at[i, j])
            copy.start()
            copies.append(copy)
    for copy in copies:
        copy.wait()


SMEM = pl.BlockSpec(memory_space=pltpu.SMEM)
VMEM = pl.BlockSpec(memory_space=pltpu.VMEM)
ANY = pl.BlockSpec(memory_space=pl.ANY)


def real_index(zhi, y, core):
    return (zhi * 4 + y) * 2 + core


def core_pairs():
    return [(r, r ^ 1) for r in range(16)]


def y_pairs(i):
    return [
        (real_index(zhi, y, c), real_index(zhi, (y + i) % 4, c)) for zhi in range(2) for y in range(4) for c in range(2)
    ]


def z_pairs():
    return [(r, (r + 8) % 16) for r in range(16)]


def edge_pairs(n):
    return [(r * n + s, r * n + (s + (1 if r % 2 else n - 1)) % n) for r in range(16) for s in range(n)]


def params(mib):
    return pltpu.CompilerParams(vmem_limit_bytes=mib * 2**20)


def halves(slots, info, pick, own, mate):
    return pl.pallas_call(
        functools.partial(half_kernel, slots),
        out_shape=jax.ShapeDtypeStruct((slots, HALF, BAND), BF),
        in_specs=[SMEM] * 2 + [ANY] * 2,
        out_specs=ANY,
        scratch_shapes=[pltpu.SemaphoreType.DMA((slots,))],
        compiler_params=params(16),
    )(info, pick, own, mate)


def cut(slots, far, info, pick, tins, band):
    win = jax.ShapeDtypeStruct((2, slots, HALF, WIN), BF)
    return pl.pallas_call(
        functools.partial(cut_kernel, slots, far),
        out_shape=[win] * 4,
        in_specs=[SMEM] * 6 + [ANY],
        out_specs=[ANY] * 4,
        scratch_shapes=[
            pltpu.VMEM((slots, HALF, BAND + WIN), BF),
            pltpu.SemaphoreType.DMA((slots, 2)),
            pltpu.SemaphoreType.DMA((slots, 8)),
        ],
        compiler_params=params(16),
    )(info, pick, *tins, band)


def select(slots, far, info, pick, group):
    return pl.pallas_call(
        functools.partial(select_kernel, slots, far),
        out_shape=[
            jax.ShapeDtypeStruct((2, PLANES, HALF, WIN), BF),
            jax.ShapeDtypeStruct((32, WIN), BF),
        ],
        in_specs=[SMEM] * 2 + [VMEM] + [ANY] * 4,
        out_specs=[VMEM] * 2,
        scratch_shapes=[pltpu.SemaphoreType.DMA((2, PLANES))],
        compiler_params=params(16),
    )(info, pick, jnp.asarray(edge_rows()), *group)


WORK = [
    pltpu.VMEM((512, 12 * 128), BF),
    pltpu.VMEM((18, 48, 256), BF),
    pltpu.VMEM((4, 3, TILES, 48, 128), F32),
]
FIELDS = (PLANES, 5, ROWS, TILES * 128)


def sample_near(scalars, mine, swapped, got, got_swapped):
    return pl.pallas_call(
        near_kernel,
        out_shape=jax.ShapeDtypeStruct(FIELDS, F32),
        in_specs=[SMEM] * 6 + [VMEM] * 5 + [ANY],
        out_specs=ANY,
        scratch_shapes=WORK + [pltpu.VMEM(FIELDS, F32), pltpu.SemaphoreType.DMA((PLANES + 1,))],
        compiler_params=params(32),
    )(*scalars, jnp.asarray(y_table()), jnp.asarray(halo_rows()), mine, swapped, got, got_swapped, jnp.asarray(x_matrix()))


def sample_far(tiles, scalars, mine, swapped, near, got=None, got_swapped=None, outs=()):
    rows = 8 * len(tiles)
    halo = got is not None
    extra = (jnp.asarray(halo_rows()), got, got_swapped) if halo else ()
    return pl.pallas_call(
        functools.partial(far_kernel, tiles, halo),
        out_shape=[
            jax.ShapeDtypeStruct((2, 1, ROWS, TILES * 128), F32),
            jax.ShapeDtypeStruct((4, 1, ROWS, TILES * 128), F32),
        ],
        in_specs=[SMEM] * 6 + [VMEM] * 2 + [ANY] * 2 + [VMEM] * len(extra) + [ANY] * len(outs),
        out_specs=[ANY] * 2,
        input_output_aliases={13: 0, 14: 1} if halo else {},
        scratch_shapes=WORK
        + [
            pltpu.VMEM((PLANES, 5, rows, TILES * 128), F32),
            pltpu.VMEM((2, 1, rows, TILES * 128), F32),
            pltpu.VMEM((4, 1, rows, TILES * 128), F32),
            pltpu.SemaphoreType.DMA((PLANES + 1, len(tiles))),
            pltpu.SemaphoreType.DMA((len(tiles), 2)),
        ],
        compiler_params=params(32),
    )(*scalars, jnp.asarray(y_table()), mine, swapped, jnp.asarray(x_matrix()), near, *extra, *outs)


def round_y(outs):
    return [outs[0]] + [lax.ppermute(outs[i], "real", y_pairs(i)) for i in range(1, 4)]


def share(parts, edges):
    swapped = lax.ppermute(parts, "real", core_pairs())
    got = lax.ppermute(edges, ("real", "sky"), edge_pairs(lax.axis_size("sky")))
    return swapped, got, lax.ppermute(got, "real", core_pairs())


def exchange(slots, scalars, pair, own, mate):
    info, pick = scalars[:2]
    half = halves(slots, info, pick, own, mate)
    other = lax.ppermute(half, "real", z_pairs())
    tins = [pair] + [lax.ppermute(pair, "real", y_pairs(i)) for i in range(1, 4)]
    parts, edges = select(slots, 0, info, pick, round_y(cut(slots, 0, info, pick, tins, half)))
    near = sample_near(scalars, parts, *share(parts, edges))
    parts, edges = select(slots, 1, info, pick, round_y(cut(slots, 1, info, pick, tins, other)))
    return near, parts, edges


def body(potential_stock, plane_pick, col_shift, mirror, subcell, lens_weight):
    mate = lax.ppermute(potential_stock, "real", core_pairs())
    me = lax.axis_index("real")
    info = jnp.stack([me // 2, me % 2]).astype(I32)
    shift, flip = col_shift[0], mirror[0]
    start = jnp.where(flip == 1, BAND - 4 - 2168 - shift, shift - 4) & (BAND - 1)
    first, rest = start // 128, start % 128
    geo = jnp.concatenate([rest, flip])
    scalars = (info, plane_pick, geo, subcell.reshape(-1), lens_weight)
    pair = jnp.concatenate([first, lax.ppermute(first, "real", core_pairs())])

    chips = plane_pick // 4
    most = jnp.max(jnp.sum((chips[:, None] == chips[None, :]).astype(I32), axis=1))
    branch = jnp.where(most <= 1, 0, jnp.where(most <= 2, 1, 2)).astype(I32)
    near, parts, edges = lax.switch(
        branch, [functools.partial(exchange, k) for k in (1, 2, 4)], scalars, pair, potential_stock, mate
    )
    swapped, got, got_swapped = share(parts, edges)
    outs = sample_far((1, 2), scalars, parts, swapped, near)
    return tuple(sample_far((0, 3), scalars, parts, swapped, near, got, got_swapped, outs))


def solution(mesh):
    return jax.shard_map(
        body,
        mesh=mesh,
        in_specs=(
            P("real", "sky", None),
            P(),
            P("real", None),
            P("real", None),
            P("sky", None),
            P(),
        ),
        out_specs=(P(None, "real", "sky", None), P(None, "real", "sky", None)),
        check_vma=False,
    )
```

```python
import functools

import jax
import jax.numpy as jnp
import numpy as np
from jax import lax
from jax.experimental import pallas as pl
from jax.experimental.pallas import tpu as pltpu
from jax.sharding import PartitionSpec as P

PLANES = 4
ROWS = 32
HALF = 16
SLOTS = 4
TILES = 16
BAND = 16384
WIN = 18 * 128
SCALE = 12288
GROUP = 8
UNROLL = 8

BF = jnp.bfloat16
F32 = jnp.float32
I32 = jnp.int32


def cubic_ints(n):
    return (
        -(n**3) + 16 * n**2 - 64 * n,
        3 * n**3 - 40 * n**2 + 1024,
        -3 * n**3 + 32 * n**2 + 64 * n,
        n**3 - 8 * n**2,
    )


def filters_1d():
    first = {-2: 1, -1: -8, 1: 8, 2: -1}
    second = {-2: -1, -1: 16, 0: -30, 1: 16, 2: -1}
    out = np.zeros((4, 3, 8), np.int64)
    for f in range(4):
        ints = cubic_ints(2 * f + 1)
        for b, w in zip(range(-1, 3), ints):
            out[f, 0, b + 3] += 12 * w
            for d, v in first.items():
                out[f, 1, b + d + 3] += v * w
            for d, v in second.items():
                out[f, 2, b + d + 3] += v * w
    return out


def x_matrix():
    taps = filters_1d()
    full = np.zeros((2, 128, 12 * 64), np.float64)
    for h in range(2):
        for f in range(4):
            for q in range(3):
                block = ((f // 2) * 3 + q) * 2 + (f + h) % 2
                for n in range(8):
                    for j in range(64):
                        full[h, j + 1 + n, block * 64 + j] = taps[f, q, n]
    high = full.astype(jnp.bfloat16).astype(np.float64)
    low = full - high
    assert np.array_equal(low.astype(jnp.bfloat16).astype(np.float64), low)
    return np.concatenate([high, low], axis=1).astype(jnp.bfloat16)


def y_table():
    taps = filters_1d().astype(np.float64) / (float(SCALE) * float(SCALE))
    return taps.astype(np.float32).reshape(-1)


def edge_rows():
    s = np.zeros((2, 32, 128), np.float32)
    for c in range(2):
        for part in range(2 * PLANES):
            for q in range(4):
                s[c, 4 * part + q, 16 * part + 12 * c + q] = 1
    return s.astype(jnp.bfloat16)


def halo_rows():
    s = np.zeros((2, 64, 64), np.float32)
    for p in range(PLANES):
        for q in range(4):
            for c in range(2):
                received, swapped = 4 * p + q, 48 + 4 * p + q
                above, below = (swapped, received) if c == 0 else (received, swapped)
                s[c, 16 * p + 4 + q, above] = 1
                s[c, 16 * p + 8 + q, below] = 1
    return s.astype(jnp.bfloat16)


def slot_planes(pick_ref, chip, slots):
    planes = [jnp.int32(-1)] * slots
    count = jnp.int32(0)
    for p in range(PLANES):
        mine = pick_ref[p] // 4 == chip
        for j in range(slots):
            planes[j] = jnp.where(mine & (count == j), p, planes[j])
        count = count + mine.astype(I32)
    return planes


def half_kernel(info, pick, own, mate, o0, o1, o2, o3, sem):
    chip, core = info[0], info[1]
    outs = (o0, o1, o2, o3)
    planes = slot_planes(pick, chip, SLOTS)
    rows = pl.ds(pl.multiple_of(core * HALF, HALF), HALF)
    for j in range(SLOTS):
        entry = pick[jnp.maximum(planes[j], 0)]
        here = (entry // 2) % 2 == core

        @pl.when((planes[j] >= 0) & here)
        def _():
            pltpu.make_async_copy(own.at[entry % 2, rows], outs[j], sem.at[j]).start()

        @pl.when((planes[j] >= 0) & jnp.logical_not(here))
        def _():
            pltpu.make_async_copy(mate.at[entry % 2, rows], outs[j], sem.at[j]).start()

    for j in range(SLOTS):

        @pl.when(planes[j] >= 0)
        def _():
            pltpu.make_async_copy(own.at[0, rows], outs[j], sem.at[j]).wait()


def cut_kernel(slot, far, info, pick, t0, t1, t2, t3, band, o0, o1, o2, o3, ext, sem_in, sem_out):
    chip = (info[0] + 4 * far) % 8
    plane = jnp.maximum(slot_planes(pick, chip, slot + 1)[slot], 0)
    tins = (t0, t1, t2, t3)
    outs = (o0, o1, o2, o3)
    fetches = (
        pltpu.make_async_copy(band, ext.at[:, pl.ds(0, BAND)], sem_in.at[0]),
        pltpu.make_async_copy(band.at[:, pl.ds(0, WIN)], ext.at[:, pl.ds(BAND, WIN)], sem_in.at[1]),
    )
    for copy in fetches:
        copy.start()
    for copy in fetches:
        copy.wait()
    copies = []
    for i in range(4):
        for e in range(2):
            tile = tins[(4 - i) % 4][e * PLANES + plane] & 127
            start = pl.multiple_of(tile * 128, 128)
            copy = pltpu.make_async_copy(ext.at[:, pl.ds(start, WIN)], outs[i].at[e], sem_out.at[2 * i + e])
            copy.start()
            copies.append(copy)
    for copy in copies:
        copy.wait()


def select_kernel(slots, info, pick, s_ref, *refs):
    groups = [refs[8 * j : 8 * j + 8] for j in range(slots)]
    parts, edges, sem = refs[8 * slots :]
    chip, core = info[0], info[1]
    zhi, y = chip // 4, chip % 4
    for p in range(PLANES):
        rank = jnp.int32(0)
        for q in range(p):
            rank = rank + (pick[q] // 4 == pick[p] // 4).astype(I32)
        owner = pick[p] // 4
        source = (y - owner % 4 + 4) % 4 + jnp.where(owner // 4 == zhi, 0, 4)
        for j in range(slots):
            for i in range(8):

                @pl.when((rank == j) & (source == i))
                def _():
                    for e in range(2):
                        pltpu.make_async_copy(groups[j][i].at[e], parts.at[e, p], sem.at[e, p]).start()

    for p in range(PLANES):
        for e in range(2):
            pltpu.make_async_copy(groups[0][0].at[0], parts.at[e, p], sem.at[e, p]).wait()
    rows = parts[...].reshape(2 * PLANES * HALF, WIN)
    edges[...] = jnp.dot(s_ref[core], rows, preferred_element_type=F32).astype(BF)


def ray_kernel(
    geo, sub, lens, ytab, halo_ref, mine, swapped, got, got_swapped, w_hbm, deflect_hbm, distort_hbm,
    deflect, distort, w_ref, view, field, sem, sem_out
):
    weights = pltpu.make_async_copy(w_hbm, w_ref, sem)
    weights.start()
    lane = lax.broadcasted_iota(I32, (16, 128), 1)
    left = lax.broadcasted_iota(I32, (1, 1, 128), 2) < 64
    core = geo[2 * PLANES]
    edge = jnp.concatenate([got[...], got_swapped[...]], axis=0)

    for k in range(PLANES):
        rest, flip = geo[k], geo[PLANES + k]
        index = jnp.where(flip == 1, rest + 127 - lane, rest + lane)
        low = index < 128
        index = index & 127
        hrow = jnp.dot(halo_ref[core, pl.ds(16 * k, 16), :], edge, preferred_element_type=F32)

        def moved(b):
            cols = pl.ds(b * 128, 128)
            m, w = mine[0, k, :, cols], swapped[1, k, :, cols]
            parts = [jnp.where(core == 0, m, w).astype(F32), jnp.where(core == 0, w, m).astype(F32)]
            parts.append(hrow[:, b * 128 : b * 128 + 128])
            return [jnp.take_along_axis(x, index, axis=1, mode="promise_in_bounds") for x in parts]

        before = moved(0)
        for b in range(17):
            after = moved(b + 1)
            c = jnp.where(flip == 1, 16 - b, b)
            for h in range(3):
                view[0, c, pl.ds(16 * h, 16), :] = jnp.where(low, before[h], after[h]).astype(BF)
            before = after
        for c in range(TILES):
            view[1, c] = jnp.concatenate([view[0, c, :, 64:], view[0, c + 1, :, :64]], axis=1)

        if k == 0:
            weights.wait()
        for g in range(TILES // GROUP):
            cs = pl.ds(g * GROUP, GROUP)
            for n in range(3):
                res = []
                for h in range(2):
                    lhs = view[h, cs].reshape(48 * GROUP, 128)
                    lhs = jnp.concatenate([lhs, lhs], axis=1)
                    out = jnp.dot(lhs, w_ref[h, :, pl.ds(n * 256, 256)], preferred_element_type=F32)
                    res.append(out.reshape(GROUP, 48, 256))
                for m in range(2):
                    pair, q = divmod(2 * n + m, 3)
                    r0, r1 = [r[:, :, m * 128 : m * 128 + 128] for r in res]
                    turned = pltpu.roll(jnp.where(left, r1, r0), 64, 2)
                    for fx, part in ((2 * pair, jnp.where(left, r0, r1)), (2 * pair + 1, turned)):
                        field[k, fx, q, cs, pl.ds(8, 32), :] = part[:, :32]
                        field[k, fx, q, cs, pl.ds(0, 8), :] = part[:, 32:40]
                        field[k, fx, q, cs, pl.ds(40, 8), :] = part[:, 40:48]

    copies = []
    for t in range(4):

        def tile(c, carry):
            o = sub[t * TILES + c]
            fx, fy = o % 4, o // 4
            wy = [[ytab[fy * 24 + q * 8 + n] for n in range(8)] for q in range(3)]
            one = jnp.ones((8, 128), F32)
            zero = jnp.zeros((8, 128), F32)
            dx, dy, a11, a12, a21, a22 = zero, zero, one, zero, zero, one
            for k in range(PLANES):

                def taps(q, lo, hi):
                    return {n: field[k, fx, q, c, pl.ds(8 * t + 5 + n, 8), :] for n in range(lo, hi)}

                def filt(vals, q, lo, hi):
                    terms = [wy[q][n] * vals[n] for n in range(lo, hi)]
                    while len(terms) > 1:
                        odd = [terms[-1]] if len(terms) % 2 else []
                        terms = [a + b for a, b in zip(terms[::2], terms[1::2])] + odd
                    return terms[0]

                s = lens[k]
                v1 = taps(1, 0, 8)
                gx = filt(v1, 0, 2, 6)
                hxy = filt(v1, 1, 0, 8) * s
                v0 = taps(0, 0, 8)
                gy = filt(v0, 1, 0, 8)
                hyy = filt(v0, 2, 0, 8) * s
                v2 = taps(2, 2, 6)
                hxx = filt(v2, 0, 2, 6) * s
                dx = dx + s * gx
                dy = dy + s * gy
                b11 = a11 - (hxx * a11 + hxy * a21)
                b12 = a12 - (hxx * a12 + hxy * a22)
                b21 = a21 - (hxy * a11 + hyy * a21)
                b22 = a22 - (hxy * a12 + hyy * a22)
                a11, a12, a21, a22 = b11, b12, b21, b22
            cols = pl.ds(pl.multiple_of(c * 128, 128), 128)
            rows = pl.ds(8 * t, 8)
            outs = (dx, dy, a11, a12, a21, a22)
            for j in range(2):
                deflect[j, 0, rows, cols] = outs[j]
            for j in range(4):
                distort[j, 0, rows, cols] = outs[2 + j]
            return carry

        lax.fori_loop(0, TILES, tile, 0, unroll=UNROLL)
        rows = pl.ds(8 * t, 8)
        for j, (src, dst) in enumerate(((deflect, deflect_hbm), (distort, distort_hbm))):
            copy = pltpu.make_async_copy(src.at[:, :, rows], dst.at[:, :, rows], sem_out.at[t, j])
            copy.start()
            copies.append(copy)
    for copy in copies:
        copy.wait()


SMEM = pl.BlockSpec(memory_space=pltpu.SMEM)
VMEM = pl.BlockSpec(memory_space=pltpu.VMEM)
ANY = pl.BlockSpec(memory_space=pl.ANY)


def real_index(zhi, y, core):
    return (zhi * 4 + y) * 2 + core


def core_pairs():
    return [(r, r ^ 1) for r in range(16)]


def y_pairs(i):
    return [
        (real_index(zhi, y, c), real_index(zhi, (y + i) % 4, c)) for zhi in range(2) for y in range(4) for c in range(2)
    ]


def z_pairs():
    return [(r, (r + 8) % 16) for r in range(16)]


def edge_pairs(n):
    return [(r * n + s, r * n + (s + (1 if r % 2 else n - 1)) % n) for r in range(16) for s in range(n)]


def params(mib):
    return pltpu.CompilerParams(vmem_limit_bytes=mib * 2**20)


def halves(info, pick, own, mate):
    return pl.pallas_call(
        half_kernel,
        out_shape=[jax.ShapeDtypeStruct((HALF, BAND), BF)] * SLOTS,
        in_specs=[SMEM] * 2 + [ANY] * 2,
        out_specs=[ANY] * SLOTS,
        scratch_shapes=[pltpu.SemaphoreType.DMA((SLOTS,))],
        compiler_params=params(16),
    )(info, pick, own, mate)


def cut(slot, far, info, pick, tins, band):
    return pl.pallas_call(
        functools.partial(cut_kernel, slot, far),
        out_shape=[jax.ShapeDtypeStruct((2, HALF, WIN), BF)] * 4,
        in_specs=[SMEM] * 6 + [ANY],
        out_specs=[ANY] * 4,
        scratch_shapes=[
            pltpu.VMEM((HALF, BAND + WIN), BF),
            pltpu.SemaphoreType.DMA((2,)),
            pltpu.SemaphoreType.DMA((8,)),
        ],
        compiler_params=params(16),
    )(info, pick, *tins, band)


def select(slots, info, pick, refs):
    return pl.pallas_call(
        functools.partial(select_kernel, slots),
        out_shape=[
            jax.ShapeDtypeStruct((2, PLANES, HALF, WIN), BF),
            jax.ShapeDtypeStruct((32, WIN), BF),
        ],
        in_specs=[SMEM] * 2 + [VMEM] + [ANY] * (8 * slots),
        out_specs=[VMEM] * 2,
        scratch_shapes=[pltpu.SemaphoreType.DMA((2, PLANES))],
        compiler_params=params(16),
    )(info, pick, jnp.asarray(edge_rows()), *refs)


def rays(geo, sub, lens, mine, swapped, got, got_swapped):
    return pl.pallas_call(
        ray_kernel,
        out_shape=[
            jax.ShapeDtypeStruct((2, 1, ROWS, TILES * 128), F32),
            jax.ShapeDtypeStruct((4, 1, ROWS, TILES * 128), F32),
        ],
        in_specs=[SMEM] * 4 + [VMEM] * 5 + [ANY],
        out_specs=[ANY] * 2,
        scratch_shapes=[
            pltpu.VMEM((2, 1, ROWS, TILES * 128), F32),
            pltpu.VMEM((4, 1, ROWS, TILES * 128), F32),
            pltpu.VMEM((2, 256, 12 * 64), BF),
            pltpu.VMEM((2, 17, 48, 128), BF),
            pltpu.VMEM((PLANES, 4, 3, TILES, 48, 128), F32),
            pltpu.SemaphoreType.DMA,
            pltpu.SemaphoreType.DMA((4, 2)),
        ],
        compiler_params=params(48),
    )(
        geo, sub, lens, jnp.asarray(y_table()), jnp.asarray(halo_rows()),
        mine, swapped, got, got_swapped, jnp.asarray(x_matrix()),
    )


def round_y(outs):
    return [outs[0]] + [lax.ppermute(outs[i], "real", y_pairs(i)) for i in range(1, 4)]


def exchange(slots, info, pick, tins, bands):
    others = [lax.ppermute(bands[j], "real", z_pairs()) for j in range(slots)]
    refs = []
    for j in range(slots):
        refs += round_y(cut(j, 0, info, pick, tins, bands[j]))
        refs += round_y(cut(j, 1, info, pick, tins, others[j]))
    return tuple(select(slots, info, pick, refs))


def body(potential_stock, plane_pick, col_shift, mirror, subcell, lens_weight):
    me = lax.axis_index("real")
    info = jnp.stack([me // 2, me % 2]).astype(I32)
    shift, flip = col_shift[0], mirror[0]
    start = jnp.where(flip == 1, BAND - 4 - 2168 - shift, shift - 4) & (BAND - 1)
    first, rest = start // 128, start % 128

    mate = lax.ppermute(potential_stock, "real", core_pairs())
    pair = jnp.concatenate([first, lax.ppermute(first, "real", core_pairs())])
    tins = [pair] + [lax.ppermute(pair, "real", y_pairs(i)) for i in range(1, 4)]

    chips = plane_pick // 4
    most = jnp.max(jnp.sum((chips[:, None] == chips[None, :]).astype(I32), axis=1))
    branch = jnp.where(most <= 1, 0, jnp.where(most <= 2, 1, 2)).astype(I32)
    parts, edges = lax.switch(
        branch,
        [functools.partial(exchange, k) for k in (1, 2, 4)],
        info, plane_pick, tins, halves(info, plane_pick, potential_stock, mate),
    )
    got = lax.ppermute(edges, ("real", "sky"), edge_pairs(lax.axis_size("sky")))
    swapped = lax.ppermute(parts, "real", core_pairs())
    got_swapped = lax.ppermute(got, "real", core_pairs())
    geo = jnp.concatenate([rest, flip, info[1:]])
    return tuple(rays(geo, subcell.reshape(-1), lens_weight, parts, swapped, got, got_swapped))


def solution(mesh):
    return jax.shard_map(
        body,
        mesh=mesh,
        in_specs=(
            P("real", "sky", None),
            P(),
            P("real", None),
            P("real", None),
            P("sky", None),
            P(),
        ),
        out_specs=(P(None, "real", "sky", None), P(None, "real", "sky", None)),
        check_vma=False,
    )
```

```python
import functools

import jax
import jax.numpy as jnp
import numpy as np
from jax import lax
from jax.experimental import pallas as pl
from jax.experimental.pallas import tpu as pltpu
from jax.sharding import PartitionSpec as P

PLANES = 4
ROWS = 32
HALF = 16
TILES = 16
BAND = 16384
WIN = 18 * 128
SCALE = 12288
GROUP = 8
UNROLL = 8

BF = jnp.bfloat16
F32 = jnp.float32
I32 = jnp.int32


def cubic_ints(n):
    return (
        -(n**3) + 16 * n**2 - 64 * n,
        3 * n**3 - 40 * n**2 + 1024,
        -3 * n**3 + 32 * n**2 + 64 * n,
        n**3 - 8 * n**2,
    )


def filters_1d():
    first = {-2: 1, -1: -8, 1: 8, 2: -1}
    second = {-2: -1, -1: 16, 0: -30, 1: 16, 2: -1}
    out = np.zeros((4, 3, 8), np.int64)
    for f in range(4):
        ints = cubic_ints(2 * f + 1)
        for b, w in zip(range(-1, 3), ints):
            out[f, 0, b + 3] += 12 * w
            for d, v in first.items():
                out[f, 1, b + d + 3] += v * w
            for d, v in second.items():
                out[f, 2, b + d + 3] += v * w
    return out


def x_matrix():
    taps = filters_1d()
    full = np.zeros((2, 128, 12 * 64), np.float64)
    for h in range(2):
        for f in range(4):
            for q in range(3):
                block = ((f // 2) * 3 + q) * 2 + (f + h) % 2
                for n in range(8):
                    for j in range(64):
                        full[h, j + 1 + n, block * 64 + j] = taps[f, q, n]
    high = full.astype(jnp.bfloat16).astype(np.float64)
    low = full - high
    assert np.array_equal(low.astype(jnp.bfloat16).astype(np.float64), low)
    return np.concatenate([high, low], axis=1).astype(jnp.bfloat16)


def y_table():
    taps = filters_1d().astype(np.float64) / (float(SCALE) * float(SCALE))
    return taps.astype(np.float32).reshape(-1)


def edge_rows():
    s = np.zeros((2, 32, 128), np.float32)
    for c in range(2):
        for part in range(2 * PLANES):
            for q in range(4):
                s[c, 4 * part + q, 16 * part + 12 * c + q] = 1
    return s.astype(jnp.bfloat16)


def halo_rows():
    s = np.zeros((2, 64, 64), np.float32)
    for p in range(PLANES):
        for q in range(4):
            for c in range(2):
                received, swapped = 4 * p + q, 48 + 4 * p + q
                above, below = (swapped, received) if c == 0 else (received, swapped)
                s[c, 16 * p + 4 + q, above] = 1
                s[c, 16 * p + 8 + q, below] = 1
    return s.astype(jnp.bfloat16)


def slot_planes(pick_ref, chip, slots):
    planes = [jnp.int32(-1)] * slots
    count = jnp.int32(0)
    for p in range(PLANES):
        mine = pick_ref[p] // 4 == chip
        for j in range(slots):
            planes[j] = jnp.where(mine & (count == j), p, planes[j])
        count = count + mine.astype(I32)
    return planes


def half_kernel(slots, info, pick, own, mate, out, sem):
    chip, core = info[0], info[1]
    planes = slot_planes(pick, chip, slots)
    rows = pl.ds(pl.multiple_of(core * HALF, HALF), HALF)
    for j in range(slots):
        entry = pick[jnp.maximum(planes[j], 0)]
        here = (planes[j] < 0) | ((entry // 2) % 2 == core)

        @pl.when(here)
        def _():
            pltpu.make_async_copy(own.at[entry % 2, rows], out.at[j], sem.at[j]).start()

        @pl.when(jnp.logical_not(here))
        def _():
            pltpu.make_async_copy(mate.at[entry % 2, rows], out.at[j], sem.at[j]).start()

    for j in range(slots):
        pltpu.make_async_copy(own.at[0, rows], out.at[j], sem.at[j]).wait()


def cut_kernel(slots, far, info, pick, t0, t1, t2, t3, band, o0, o1, o2, o3, ext, sem_in, sem_out):
    chip = (info[0] + 4 * far) % 8
    planes = slot_planes(pick, chip, slots)
    tins = (t0, t1, t2, t3)
    outs = (o0, o1, o2, o3)
    fetches = []
    for j in range(slots):
        fetches.append((
            pltpu.make_async_copy(band.at[j], ext.at[j, :, pl.ds(0, BAND)], sem_in.at[j, 0]),
            pltpu.make_async_copy(band.at[j, :, pl.ds(0, WIN)], ext.at[j, :, pl.ds(BAND, WIN)], sem_in.at[j, 1]),
        ))
        for copy in fetches[j]:
            copy.start()
    copies = []
    for j in range(slots):
        for copy in fetches[j]:
            copy.wait()
        plane = jnp.maximum(planes[j], 0)
        for i in range(4):
            for e in range(2):
                tile = tins[(4 - i) % 4][e * PLANES + plane] & 127
                start = pl.multiple_of(tile * 128, 128)
                copy = pltpu.make_async_copy(
                    ext.at[j, :, pl.ds(start, WIN)], outs[i].at[e, j], sem_out.at[j, 2 * i + e]
                )
                copy.start()
                copies.append(copy)
    for copy in copies:
        copy.wait()


def select_kernel(slots, info, pick, s_ref, *refs):
    near, far = refs[:4], refs[4:8]
    parts, edges, sem = refs[8:]
    chip, core = info[0], info[1]
    zhi, y = chip // 4, chip % 4
    for p in range(PLANES):
        rank = jnp.int32(0)
        for q in range(p):
            rank = rank + (pick[q] // 4 == pick[p] // 4).astype(I32)
        rank = rank if slots > 1 else 0
        owner = pick[p] // 4
        step = (y - owner % 4 + 4) % 4
        same = owner // 4 == zhi
        for i in range(4):
            for group, here in ((near, same), (far, jnp.logical_not(same))):

                @pl.when(here & (step == i))
                def _():
                    for e in range(2):
                        pltpu.make_async_copy(group[i].at[e, rank], parts.at[e, p], sem.at[e, p]).start()

    for p in range(PLANES):
        for e in range(2):
            pltpu.make_async_copy(near[0].at[0, 0], parts.at[e, p], sem.at[e, p]).wait()
    rows = parts[...].reshape(2 * PLANES * HALF, WIN)
    edges[...] = jnp.dot(s_ref[core], rows, preferred_element_type=F32).astype(BF)


def ray_kernel(
    geo, sub, lens, ytab, halo_ref, mine, swapped, got, got_swapped, w_hbm, deflect_hbm, distort_hbm,
    deflect, distort, w_ref, view, field, sem, sem_out
):
    weights = pltpu.make_async_copy(w_hbm, w_ref, sem)
    weights.start()
    lane = lax.broadcasted_iota(I32, (16, 128), 1)
    left = lax.broadcasted_iota(I32, (1, 1, 128), 2) < 64
    core = geo[2 * PLANES]
    edge = jnp.concatenate([got[...], got_swapped[...]], axis=0)

    def plane(k, carry):
        rest, flip = geo[k], geo[PLANES + k]
        index = jnp.where(flip == 1, rest + 127 - lane, rest + lane)
        low = index < 128
        index = index & 127
        hrow = jnp.dot(halo_ref[core, pl.ds(pl.multiple_of(16 * k, 16), 16), :], edge, preferred_element_type=F32)

        def moved(b):
            cols = pl.ds(b * 128, 128)
            m, w = mine[0, k, :, cols], swapped[1, k, :, cols]
            parts = [jnp.where(core == 0, m, w).astype(F32), jnp.where(core == 0, w, m).astype(F32)]
            parts.append(hrow[:, b * 128 : b * 128 + 128])
            return [jnp.take_along_axis(x, index, axis=1, mode="promise_in_bounds") for x in parts]

        before = moved(0)
        for b in range(17):
            after = moved(b + 1)
            c = jnp.where(flip == 1, 16 - b, b)
            for h in range(3):
                view[0, c, pl.ds(16 * h, 16), :] = jnp.where(low, before[h], after[h]).astype(BF)
            before = after
        for c in range(TILES):
            view[1, c] = jnp.concatenate([view[0, c, :, 64:], view[0, c + 1, :, :64]], axis=1)

        for g in range(TILES // GROUP):
            cs = pl.ds(g * GROUP, GROUP)
            for n in range(3):
                res = []
                for h in range(2):
                    lhs = view[h, cs].reshape(48 * GROUP, 128)
                    lhs = jnp.concatenate([lhs, lhs], axis=1)
                    out = jnp.dot(lhs, w_ref[h, :, pl.ds(n * 256, 256)], preferred_element_type=F32)
                    res.append(out.reshape(GROUP, 48, 256))
                for m in range(2):
                    pair, q = divmod(2 * n + m, 3)
                    r0, r1 = [r[:, :, m * 128 : m * 128 + 128] for r in res]
                    turned = pltpu.roll(jnp.where(left, r1, r0), 64, 2)
                    for fx, part in ((2 * pair, jnp.where(left, r0, r1)), (2 * pair + 1, turned)):
                        field[k, fx, q, cs, pl.ds(8, 32), :] = part[:, :32]
                        field[k, fx, q, cs, pl.ds(0, 8), :] = part[:, 32:40]
                        field[k, fx, q, cs, pl.ds(40, 8), :] = part[:, 40:48]
        return carry

    weights.wait()
    lax.fori_loop(0, PLANES, plane, 0)

    copies = []
    for t in range(4):

        def tile(c, carry):
            o = sub[t * TILES + c]
            fx, fy = o % 4, o // 4
            wy = [[ytab[fy * 24 + q * 8 + n] for n in range(8)] for q in range(3)]
            one = jnp.ones((8, 128), F32)
            zero = jnp.zeros((8, 128), F32)
            dx, dy, a11, a12, a21, a22 = zero, zero, one, zero, zero, one
            for k in range(PLANES):

                def taps(q, lo, hi):
                    return {n: field[k, fx, q, c, pl.ds(8 * t + 5 + n, 8), :] for n in range(lo, hi)}

                def filt(vals, q, lo, hi):
                    terms = [wy[q][n] * vals[n] for n in range(lo, hi)]
                    while len(terms) > 1:
                        odd = [terms[-1]] if len(terms) % 2 else []
                        terms = [a + b for a, b in zip(terms[::2], terms[1::2])] + odd
                    return terms[0]

                s = lens[k]
                v1 = taps(1, 0, 8)
                gx = filt(v1, 0, 2, 6)
                hxy = filt(v1, 1, 0, 8) * s
                v0 = taps(0, 0, 8)
                gy = filt(v0, 1, 0, 8)
                hyy = filt(v0, 2, 0, 8) * s
                v2 = taps(2, 2, 6)
                hxx = filt(v2, 0, 2, 6) * s
                dx = dx + s * gx
                dy = dy + s * gy
                b11 = a11 - (hxx * a11 + hxy * a21)
                b12 = a12 - (hxx * a12 + hxy * a22)
                b21 = a21 - (hxy * a11 + hyy * a21)
                b22 = a22 - (hxy * a12 + hyy * a22)
                a11, a12, a21, a22 = b11, b12, b21, b22
            cols = pl.ds(pl.multiple_of(c * 128, 128), 128)
            rows = pl.ds(8 * t, 8)
            outs = (dx, dy, a11, a12, a21, a22)
            for j in range(2):
                deflect[j, 0, rows, cols] = outs[j]
            for j in range(4):
                distort[j, 0, rows, cols] = outs[2 + j]
            return carry

        lax.fori_loop(0, TILES, tile, 0, unroll=UNROLL)
        rows = pl.ds(8 * t, 8)
        for j, (src, dst) in enumerate(((deflect, deflect_hbm), (distort, distort_hbm))):
            copy = pltpu.make_async_copy(src.at[:, :, rows], dst.at[:, :, rows], sem_out.at[t, j])
            copy.start()
            copies.append(copy)
    for copy in copies:
        copy.wait()


SMEM = pl.BlockSpec(memory_space=pltpu.SMEM)
VMEM = pl.BlockSpec(memory_space=pltpu.VMEM)
ANY = pl.BlockSpec(memory_space=pl.ANY)


def real_index(zhi, y, core):
    return (zhi * 4 + y) * 2 + core


def core_pairs():
    return [(r, r ^ 1) for r in range(16)]


def y_pairs(i):
    return [
        (real_index(zhi, y, c), real_index(zhi, (y + i) % 4, c)) for zhi in range(2) for y in range(4) for c in range(2)
    ]


def z_pairs():
    return [(r, (r + 8) % 16) for r in range(16)]


def edge_pairs(n):
    return [(r * n + s, r * n + (s + (1 if r % 2 else n - 1)) % n) for r in range(16) for s in range(n)]


def params(mib):
    return pltpu.CompilerParams(vmem_limit_bytes=mib * 2**20)


def halves(slots, info, pick, own, mate):
    return pl.pallas_call(
        functools.partial(half_kernel, slots),
        out_shape=jax.ShapeDtypeStruct((slots, HALF, BAND), BF),
        in_specs=[SMEM] * 2 + [ANY] * 2,
        out_specs=ANY,
        scratch_shapes=[pltpu.SemaphoreType.DMA((slots,))],
        compiler_params=params(16),
    )(info, pick, own, mate)


def cut(slots, far, info, pick, tins, band):
    win = jax.ShapeDtypeStruct((2, slots, HALF, WIN), BF)
    return pl.pallas_call(
        functools.partial(cut_kernel, slots, far),
        out_shape=[win] * 4,
        in_specs=[SMEM] * 6 + [ANY],
        out_specs=[ANY] * 4,
        scratch_shapes=[
            pltpu.VMEM((slots, HALF, BAND + WIN), BF),
            pltpu.SemaphoreType.DMA((slots, 2)),
            pltpu.SemaphoreType.DMA((slots, 8)),
        ],
        compiler_params=params(16),
    )(info, pick, *tins, band)


def select(slots, info, pick, near, far):
    return pl.pallas_call(
        functools.partial(select_kernel, slots),
        out_shape=[
            jax.ShapeDtypeStruct((2, PLANES, HALF, WIN), BF),
            jax.ShapeDtypeStruct((32, WIN), BF),
        ],
        in_specs=[SMEM] * 2 + [VMEM] + [ANY] * 8,
        out_specs=[VMEM] * 2,
        scratch_shapes=[pltpu.SemaphoreType.DMA((2, PLANES))],
        compiler_params=params(16),
    )(info, pick, jnp.asarray(edge_rows()), *near, *far)


def rays(geo, sub, lens, mine, swapped, got, got_swapped):
    return pl.pallas_call(
        ray_kernel,
        out_shape=[
            jax.ShapeDtypeStruct((2, 1, ROWS, TILES * 128), F32),
            jax.ShapeDtypeStruct((4, 1, ROWS, TILES * 128), F32),
        ],
        in_specs=[SMEM] * 4 + [VMEM] * 5 + [ANY],
        out_specs=[ANY] * 2,
        scratch_shapes=[
            pltpu.VMEM((2, 1, ROWS, TILES * 128), F32),
            pltpu.VMEM((4, 1, ROWS, TILES * 128), F32),
            pltpu.VMEM((2, 256, 12 * 64), BF),
            pltpu.VMEM((2, 17, 48, 128), BF),
            pltpu.VMEM((PLANES, 4, 3, TILES, 48, 128), F32),
            pltpu.SemaphoreType.DMA,
            pltpu.SemaphoreType.DMA((4, 2)),
        ],
        compiler_params=params(48),
    )(
        geo, sub, lens, jnp.asarray(y_table()), jnp.asarray(halo_rows()),
        mine, swapped, got, got_swapped, jnp.asarray(x_matrix()),
    )


def round_y(outs):
    return [outs[0]] + [lax.ppermute(outs[i], "real", y_pairs(i)) for i in range(1, 4)]


def exchange(slots, info, pick, pair, own, mate, half):
    if slots > 1:
        half = halves(slots, info, pick, own, mate)
    other = lax.ppermute(half, "real", z_pairs())
    tins = [pair] + [lax.ppermute(pair, "real", y_pairs(i)) for i in range(1, 4)]
    near = round_y(cut(slots, 0, info, pick, tins, half))
    far = round_y(cut(slots, 1, info, pick, tins, other))
    return tuple(select(slots, info, pick, near, far))


def body(potential_stock, plane_pick, col_shift, mirror, subcell, lens_weight):
    me = lax.axis_index("real")
    info = jnp.stack([me // 2, me % 2]).astype(I32)
    shift, flip = col_shift[0], mirror[0]
    start = jnp.where(flip == 1, BAND - 4 - 2168 - shift, shift - 4) & (BAND - 1)
    first, rest = start // 128, start % 128

    mate = lax.ppermute(potential_stock, "real", core_pairs())
    pair = jnp.concatenate([first, lax.ppermute(first, "real", core_pairs())])
    half = halves(1, info, plane_pick, potential_stock, mate)

    chips = plane_pick // 4
    most = jnp.max(jnp.sum((chips[:, None] == chips[None, :]).astype(I32), axis=1))
    branch = jnp.where(most <= 1, 0, jnp.where(most <= 2, 1, 2)).astype(I32)
    parts, edges = lax.switch(
        branch,
        [functools.partial(exchange, k) for k in (1, 2, 4)],
        info, plane_pick, pair, potential_stock, mate, half,
    )
    got = lax.ppermute(edges, ("real", "sky"), edge_pairs(lax.axis_size("sky")))
    swapped = lax.ppermute(parts, "real", core_pairs())
    got_swapped = lax.ppermute(got, "real", core_pairs())
    geo = jnp.concatenate([rest, flip, info[1:]])
    return tuple(rays(geo, subcell.reshape(-1), lens_weight, parts, swapped, got, got_swapped))


def solution(mesh):
    return jax.shard_map(
        body,
        mesh=mesh,
        in_specs=(
            P("real", "sky", None),
            P(),
            P("real", None),
            P("real", None),
            P("sky", None),
            P(),
        ),
        out_specs=(P(None, "real", "sky", None), P(None, "real", "sky", None)),
        check_vma=False,
    )
```

```python
import functools

import jax
import jax.numpy as jnp
import numpy as np
from jax import lax
from jax.experimental import pallas as pl
from jax.experimental.pallas import tpu as pltpu
from jax.sharding import PartitionSpec as P

PLANES = 4
ROWS = 32
HALF = 16
TILES = 16
BAND = 16384
WIN = 18 * 128
SCALE = 12288
GROUP = 8
UNROLL = 8

BF = jnp.bfloat16
F32 = jnp.float32
I32 = jnp.int32


def cubic_ints(n):
    return (
        -(n**3) + 16 * n**2 - 64 * n,
        3 * n**3 - 40 * n**2 + 1024,
        -3 * n**3 + 32 * n**2 + 64 * n,
        n**3 - 8 * n**2,
    )


def filters_1d():
    first = {-2: 1, -1: -8, 1: 8, 2: -1}
    second = {-2: -1, -1: 16, 0: -30, 1: 16, 2: -1}
    out = np.zeros((4, 3, 8), np.int64)
    for f in range(4):
        ints = cubic_ints(2 * f + 1)
        for b, w in zip(range(-1, 3), ints):
            out[f, 0, b + 3] += 12 * w
            for d, v in first.items():
                out[f, 1, b + d + 3] += v * w
            for d, v in second.items():
                out[f, 2, b + d + 3] += v * w
    return out


def x_matrix():
    taps = filters_1d()
    full = np.zeros((2, 128, 12 * 64), np.float64)
    for h in range(2):
        for f in range(4):
            for q in range(3):
                block = ((f // 2) * 3 + q) * 2 + (f + h) % 2
                for n in range(8):
                    for j in range(64):
                        full[h, j + 1 + n, block * 64 + j] = taps[f, q, n]
    high = full.astype(jnp.bfloat16).astype(np.float64)
    low = full - high
    assert np.array_equal(low.astype(jnp.bfloat16).astype(np.float64), low)
    return np.concatenate([high, low], axis=1).astype(jnp.bfloat16)


def y_table():
    taps = filters_1d().astype(np.float64) / (float(SCALE) * float(SCALE))
    return taps.astype(np.float32).reshape(-1)


def edge_count(parts):
    return -(-4 * parts // 16) * 16


def edge_rows(parts):
    s = np.zeros((2, edge_count(parts), HALF * parts), np.float32)
    for c in range(2):
        for part in range(parts):
            for q in range(4):
                s[c, 4 * part + q, HALF * part + 12 * c + q] = 1
    return s.astype(jnp.bfloat16)


def slot_planes(pick_ref, chip, slots):
    planes = [jnp.int32(-1)] * slots
    count = jnp.int32(0)
    for p in range(PLANES):
        mine = pick_ref[p] // 4 == chip
        for j in range(slots):
            planes[j] = jnp.where(mine & (count == j), p, planes[j])
        count = count + mine.astype(I32)
    return planes


def half_kernel(slots, info, pick, own, mate, out, sem):
    chip, core = info[0], info[1]
    planes = slot_planes(pick, chip, slots)
    rows = pl.ds(pl.multiple_of(core * HALF, HALF), HALF)
    for j in range(slots):
        entry = pick[jnp.maximum(planes[j], 0)]
        here = (planes[j] < 0) | ((entry // 2) % 2 == core)

        @pl.when(here)
        def _():
            pltpu.make_async_copy(own.at[entry % 2, rows], out.at[j], sem.at[j]).start()

        @pl.when(jnp.logical_not(here))
        def _():
            pltpu.make_async_copy(mate.at[entry % 2, rows], out.at[j], sem.at[j]).start()

    for j in range(slots):
        pltpu.make_async_copy(own.at[0, rows], out.at[j], sem.at[j]).wait()


def cut_kernel(slots, info, pick, t0, t1, t2, t3, band, o0, o1, o2, o3, ext, sem_in, sem_out):
    planes = slot_planes(pick, info[0], slots)
    tins = (t0, t1, t2, t3)
    outs = (o0, o1, o2, o3)
    fetches = []
    for j in range(slots):
        fetches.append((
            pltpu.make_async_copy(band.at[j], ext.at[j, :, pl.ds(0, BAND)], sem_in.at[j, 0]),
            pltpu.make_async_copy(band.at[j, :, pl.ds(0, WIN)], ext.at[j, :, pl.ds(BAND, WIN)], sem_in.at[j, 1]),
        ))
        for copy in fetches[j]:
            copy.start()
    copies = []
    for j in range(slots):
        for copy in fetches[j]:
            copy.wait()
        plane = jnp.maximum(planes[j], 0)
        for i in range(4):
            for f in range(2):
                for e in range(2):
                    tile = tins[(4 - i) % 4][8 * f + e * PLANES + plane] & 127
                    start = pl.multiple_of(tile * 128, 128)
                    copy = pltpu.make_async_copy(
                        ext.at[j, :, pl.ds(start, WIN)], outs[i].at[f, e, j], sem_out.at[j, 4 * i + 2 * f + e]
                    )
                    copy.start()
                    copies.append(copy)
    for copy in copies:
        copy.wait()


def half_rank(pick, p):
    rank = jnp.int32(0)
    for q in range(p):
        rank = rank + (pick[q] // 16 == pick[p] // 16).astype(I32)
    return rank


def select_kernel(slots, n, info, pick, s_near, s_far, r0, r1, r2, r3, near, send, edges, sem):
    chip, core = info[0], info[1]
    zhi, y = chip // 4, chip % 4
    group = (r0, r1, r2, r3)
    count = jnp.int32(0)
    for p in range(PLANES):
        rank = jnp.int32(0)
        for q in range(p):
            rank = rank + (pick[q] // 4 == pick[p] // 4).astype(I32)
        rank = rank if slots > 1 else 0
        owner = pick[p] // 4
        step = (y - owner % 4 + 4) % 4
        here = owner // 4 == zhi
        count = count + here.astype(I32)
        place = jnp.minimum(half_rank(pick, p), n - 1)
        for i in range(4):

            @pl.when(here & (step == i))
            def _():
                for e in range(2):
                    pltpu.make_async_copy(group[i].at[0, e, rank], near.at[e, p], sem.at[0, e, p]).start()
                    pltpu.make_async_copy(group[i].at[1, e, rank], send.at[place, e], sem.at[1, e, p]).start()

        @pl.when(jnp.logical_not(here))
        def _():
            near[:, p] = jnp.zeros((2, HALF, WIN), BF)

    for j in range(n):

        @pl.when(count <= j)
        def _():
            send[j] = jnp.zeros((2, HALF, WIN), BF)

    for p in range(PLANES):

        @pl.when(pick[p] // 16 == zhi)
        def _():
            for f in range(2):
                for e in range(2):
                    pltpu.make_async_copy(r0.at[0, 0, 0], near.at[e, p], sem.at[f, e, p]).wait()

    edges[pl.ds(0, 32), :] = jnp.dot(
        s_near[core], near[...].reshape(2 * PLANES * HALF, WIN), preferred_element_type=F32
    ).astype(BF)
    edges[pl.ds(32, edge_count(2 * n)), :] = jnp.dot(
        s_far[core], send[...].reshape(2 * n * HALF, WIN), preferred_element_type=F32
    ).astype(BF)


def gather_kernel(n, info, pick, near, near_w, far, far_w, got, got_w, gotf, main, halo, gotf_w, sem, sem_edge):
    chip, core = info[0], info[1]
    zhi = chip // 4
    mine = pl.ds(pl.multiple_of(core * HALF, HALF), HALF)
    others = pl.ds(pl.multiple_of((1 - core) * HALF, HALF), HALF)
    nf = edge_count(2 * n)
    fetch = pltpu.make_async_copy(far_w.at[pl.ds(n * HALF, nf)], gotf_w, sem_edge)
    fetch.start()
    for p in range(PLANES):
        here = pick[p] // 16 == zhi
        place = jnp.minimum(half_rank(pick, p), n - 1)

        @pl.when(here)
        def _():
            pltpu.make_async_copy(near.at[0, p], main.at[p, mine], sem.at[p, 0]).start()
            pltpu.make_async_copy(near_w.at[1, p], main.at[p, others], sem.at[p, 1]).start()

        @pl.when(jnp.logical_not(here))
        def _():
            pltpu.make_async_copy(far.at[place, 0], main.at[p, mine], sem.at[p, 0]).start()
            rows = pl.ds(pl.multiple_of(place * HALF, HALF), HALF)
            pltpu.make_async_copy(far_w.at[rows], main.at[p, others], sem.at[p, 1]).start()

    fetch.wait()
    edge = jnp.concatenate([got[...], got_w[...], gotf[...], gotf_w[...]], axis=0)
    for p in range(PLANES):
        here = pick[p] // 16 == zhi
        place = jnp.minimum(half_rank(pick, p), n - 1)
        received = jnp.where(here, 4 * p, 2 * (32 + nf) + 8 * place)
        swapped = jnp.where(here, 32 + nf + 16 + 4 * p, 2 * (32 + nf) + nf + 8 * place + 4)
        above = jnp.where(core == 0, swapped, received)
        below = jnp.where(core == 0, received, swapped)
        row = lax.broadcasted_iota(I32, (16, edge.shape[0]), 0)
        col = lax.broadcasted_iota(I32, (16, edge.shape[0]), 1)
        wanted = jnp.where(row < 8, above + row - 4, below + row - 8)
        hit = (row >= 4) & (row < 12) & (col == wanted)
        pick_rows = jnp.where(hit, 1.0, 0.0).astype(BF)
        halo[pl.ds(16 * p, 16), :] = jnp.dot(pick_rows, edge, preferred_element_type=F32).astype(BF)

    for p in range(PLANES):
        pltpu.make_async_copy(near.at[0, 0], main.at[p, mine], sem.at[p, 0]).wait()
        pltpu.make_async_copy(near.at[0, 0], main.at[p, others], sem.at[p, 1]).wait()


def whole_kernel(first, bands, main, ext, sem):
    for p in range(PLANES):
        fetches = (
            pltpu.make_async_copy(bands.at[p], ext.at[:, pl.ds(0, BAND)], sem.at[0]),
            pltpu.make_async_copy(bands.at[p, :, pl.ds(0, WIN)], ext.at[:, pl.ds(BAND, WIN)], sem.at[1]),
        )
        for copy in fetches:
            copy.start()
        for copy in fetches:
            copy.wait()
        start = pl.multiple_of((first[p] & 127) * 128, 128)
        copy = pltpu.make_async_copy(ext.at[:, pl.ds(start, WIN)], main.at[p], sem.at[2])
        copy.start()
        copy.wait()


def ray_kernel(
    geo, sub, lens, ytab, main, halo, w_hbm, deflect_hbm, distort_hbm,
    deflect, distort, w_ref, view, field, sem, sem_out
):
    weights = pltpu.make_async_copy(w_hbm, w_ref, sem)
    weights.start()
    lane = lax.broadcasted_iota(I32, (16, 128), 1)
    left = lax.broadcasted_iota(I32, (1, 1, 128), 2) < 64

    def plane(k, carry):
        rest, flip = geo[k], geo[PLANES + k]
        index = jnp.where(flip == 1, rest + 127 - lane, rest + lane)
        low = index < 128
        index = index & 127
        def moved(b):
            cols = pl.ds(b * 128, 128)
            parts = [main[k, pl.ds(16 * h, 16), cols].astype(F32) for h in range(2)]
            parts.append(halo[pl.ds(pl.multiple_of(16 * k, 16), 16), cols].astype(F32))
            return [jnp.take_along_axis(x, index, axis=1, mode="promise_in_bounds") for x in parts]

        before = moved(0)
        for b in range(17):
            after = moved(b + 1)
            c = jnp.where(flip == 1, 16 - b, b)
            for h in range(3):
                view[0, c, pl.ds(16 * h, 16), :] = jnp.where(low, before[h], after[h]).astype(BF)
            before = after
        for c in range(TILES):
            view[1, c] = jnp.concatenate([view[0, c, :, 64:], view[0, c + 1, :, :64]], axis=1)

        for g in range(TILES // GROUP):
            cs = pl.ds(g * GROUP, GROUP)
            for n in range(3):
                res = []
                for h in range(2):
                    lhs = view[h, cs].reshape(48 * GROUP, 128)
                    lhs = jnp.concatenate([lhs, lhs], axis=1)
                    out = jnp.dot(lhs, w_ref[h, :, pl.ds(n * 256, 256)], preferred_element_type=F32)
                    res.append(out.reshape(GROUP, 48, 256))
                for m in range(2):
                    pair, q = divmod(2 * n + m, 3)
                    r0, r1 = [r[:, :, m * 128 : m * 128 + 128] for r in res]
                    turned = pltpu.roll(jnp.where(left, r1, r0), 64, 2)
                    for fx, part in ((2 * pair, jnp.where(left, r0, r1)), (2 * pair + 1, turned)):
                        field[k, fx, q, cs, pl.ds(8, 32), :] = part[:, :32]
                        field[k, fx, q, cs, pl.ds(0, 8), :] = part[:, 32:40]
                        field[k, fx, q, cs, pl.ds(40, 8), :] = part[:, 40:48]
        return carry

    weights.wait()
    lax.fori_loop(0, PLANES, plane, 0)

    copies = []
    for t in range(4):

        def tile(c, carry):
            o = sub[t * TILES + c]
            fx, fy = o % 4, o // 4
            wy = [[ytab[fy * 24 + q * 8 + n] for n in range(8)] for q in range(3)]
            one = jnp.ones((8, 128), F32)
            zero = jnp.zeros((8, 128), F32)
            dx, dy, a11, a12, a21, a22 = zero, zero, one, zero, zero, one
            for k in range(PLANES):

                def taps(q, lo, hi):
                    return {n: field[k, fx, q, c, pl.ds(8 * t + 5 + n, 8), :] for n in range(lo, hi)}

                def filt(vals, q, lo, hi):
                    terms = [wy[q][n] * vals[n] for n in range(lo, hi)]
                    while len(terms) > 1:
                        odd = [terms[-1]] if len(terms) % 2 else []
                        terms = [a + b for a, b in zip(terms[::2], terms[1::2])] + odd
                    return terms[0]

                s = lens[k]
                v1 = taps(1, 0, 8)
                gx = filt(v1, 0, 2, 6)
                hxy = filt(v1, 1, 0, 8) * s
                v0 = taps(0, 0, 8)
                gy = filt(v0, 1, 0, 8)
                hyy = filt(v0, 2, 0, 8) * s
                v2 = taps(2, 2, 6)
                hxx = filt(v2, 0, 2, 6) * s
                dx = dx + s * gx
                dy = dy + s * gy
                b11 = a11 - (hxx * a11 + hxy * a21)
                b12 = a12 - (hxx * a12 + hxy * a22)
                b21 = a21 - (hxy * a11 + hyy * a21)
                b22 = a22 - (hxy * a12 + hyy * a22)
                a11, a12, a21, a22 = b11, b12, b21, b22
            cols = pl.ds(pl.multiple_of(c * 128, 128), 128)
            rows = pl.ds(8 * t, 8)
            outs = (dx, dy, a11, a12, a21, a22)
            for j in range(2):
                deflect[j, 0, rows, cols] = outs[j]
            for j in range(4):
                distort[j, 0, rows, cols] = outs[2 + j]
            return carry

        lax.fori_loop(0, TILES, tile, 0, unroll=UNROLL)
        rows = pl.ds(8 * t, 8)
        for j, (src, dst) in enumerate(((deflect, deflect_hbm), (distort, distort_hbm))):
            copy = pltpu.make_async_copy(src.at[:, :, rows], dst.at[:, :, rows], sem_out.at[t, j])
            copy.start()
            copies.append(copy)
    for copy in copies:
        copy.wait()


SMEM = pl.BlockSpec(memory_space=pltpu.SMEM)
VMEM = pl.BlockSpec(memory_space=pltpu.VMEM)
ANY = pl.BlockSpec(memory_space=pl.ANY)


def real_index(zhi, y, core):
    return (zhi * 4 + y) * 2 + core


def core_pairs():
    return [(r, r ^ 1) for r in range(16)]


def y_pairs(i):
    return [
        (real_index(zhi, y, c), real_index(zhi, (y + i) % 4, c)) for zhi in range(2) for y in range(4) for c in range(2)
    ]


def z_pairs():
    return [(r, (r + 8) % 16) for r in range(16)]


def edge_pairs(n):
    return [(r * n + s, r * n + (s + (1 if r % 2 else n - 1)) % n) for r in range(16) for s in range(n)]


def params(mib):
    return pltpu.CompilerParams(vmem_limit_bytes=mib * 2**20)


def halves(slots, info, pick, own, mate):
    return pl.pallas_call(
        functools.partial(half_kernel, slots),
        out_shape=jax.ShapeDtypeStruct((slots, HALF, BAND), BF),
        in_specs=[SMEM] * 2 + [ANY] * 2,
        out_specs=ANY,
        scratch_shapes=[pltpu.SemaphoreType.DMA((slots,))],
        compiler_params=params(16),
    )(info, pick, own, mate)


def cut(slots, info, pick, tins, band):
    win = jax.ShapeDtypeStruct((2, 2, slots, HALF, WIN), BF)
    return pl.pallas_call(
        functools.partial(cut_kernel, slots),
        out_shape=[win] * 4,
        in_specs=[SMEM] * 6 + [ANY],
        out_specs=[ANY] * 4,
        scratch_shapes=[
            pltpu.VMEM((slots, HALF, BAND + WIN), BF),
            pltpu.SemaphoreType.DMA((slots, 2)),
            pltpu.SemaphoreType.DMA((slots, 16)),
        ],
        compiler_params=params(16),
    )(info, pick, *tins, band)


def select(slots, n, info, pick, group):
    return pl.pallas_call(
        functools.partial(select_kernel, slots, n),
        out_shape=[
            jax.ShapeDtypeStruct((2, PLANES, HALF, WIN), BF),
            jax.ShapeDtypeStruct((n, 2, HALF, WIN), BF),
            jax.ShapeDtypeStruct((32 + edge_count(2 * n), WIN), BF),
        ],
        in_specs=[SMEM] * 2 + [VMEM] * 2 + [ANY] * 4,
        out_specs=[VMEM] * 3,
        scratch_shapes=[pltpu.SemaphoreType.DMA((2, 2, PLANES))],
        compiler_params=params(16),
    )(info, pick, jnp.asarray(edge_rows(2 * PLANES)), jnp.asarray(edge_rows(2 * n)), *group)


def gather(n, info, pick, *arrays):
    return pl.pallas_call(
        functools.partial(gather_kernel, n),
        out_shape=[jax.ShapeDtypeStruct((PLANES, ROWS, WIN), BF), jax.ShapeDtypeStruct((64, WIN), BF)],
        in_specs=[SMEM] * 2 + [ANY] * 4 + [VMEM] * 3,
        out_specs=[VMEM] * 2,
        scratch_shapes=[
            pltpu.VMEM((edge_count(2 * n), WIN), BF),
            pltpu.SemaphoreType.DMA((PLANES, 2)),
            pltpu.SemaphoreType.DMA,
        ],
        compiler_params=params(16),
    )(info, pick, *arrays)


def windows(first, bands):
    return pl.pallas_call(
        whole_kernel,
        out_shape=jax.ShapeDtypeStruct((PLANES, ROWS, WIN), BF),
        in_specs=[SMEM, ANY],
        out_specs=ANY,
        scratch_shapes=[pltpu.VMEM((ROWS, BAND + WIN), BF), pltpu.SemaphoreType.DMA((3,))],
        compiler_params=params(16),
    )(first, bands)


def rays(geo, sub, lens, main, halo):
    return pl.pallas_call(
        ray_kernel,
        out_shape=[
            jax.ShapeDtypeStruct((2, 1, ROWS, TILES * 128), F32),
            jax.ShapeDtypeStruct((4, 1, ROWS, TILES * 128), F32),
        ],
        in_specs=[SMEM] * 4 + [VMEM] * 2 + [ANY],
        out_specs=[ANY] * 2,
        scratch_shapes=[
            pltpu.VMEM((2, 1, ROWS, TILES * 128), F32),
            pltpu.VMEM((4, 1, ROWS, TILES * 128), F32),
            pltpu.VMEM((2, 256, 12 * 64), BF),
            pltpu.VMEM((2, 17, 48, 128), BF),
            pltpu.VMEM((PLANES, 4, 3, TILES, 48, 128), F32),
            pltpu.SemaphoreType.DMA,
            pltpu.SemaphoreType.DMA((4, 2)),
        ],
        compiler_params=params(48),
    )(geo, sub, lens, jnp.asarray(y_table()), main, halo, jnp.asarray(x_matrix()))


def swap(x):
    return lax.ppermute(x, "real", core_pairs())


def exchange(slots, n, info, pick, first, tins, own, mate, half):
    if slots > 1:
        half = halves(slots, info, pick, own, mate)
    outs = cut(slots, info, pick, tins, half)
    group = [outs[0]] + [lax.ppermute(outs[i], "real", y_pairs(i)) for i in range(1, 4)]
    near, send, edges = select(slots, n, info, pick, group)
    far = lax.ppermute(send, "real", z_pairs())
    got = lax.ppermute(edges, ("real", "sky"), edge_pairs(lax.axis_size("sky")))
    got_far = lax.ppermute(got[32:], "real", z_pairs())
    packed = jnp.concatenate([far[:, 1].reshape(n * HALF, WIN), got_far], axis=0)
    return tuple(gather(n, info, pick, near, swap(near), far, swap(packed), got, swap(got), got_far))


def any_picks(info, pick, first, tins, own, mate, half):
    me = lax.axis_index("real")
    kept = [
        jnp.where(pick[p] // 2 == me, lax.dynamic_index_in_dim(own, pick[p] % 2, 0, keepdims=False), 0)
        for p in range(PLANES)
    ]
    bands = jnp.stack(kept).astype(BF)
    for bit in (1, 2, 4, 8):
        bands = bands + lax.ppermute(bands, "real", [(r, r ^ bit) for r in range(16)])
    main = windows(first, bands)
    n = lax.axis_size("sky")
    up = lax.ppermute(main[:, ROWS - 4 :], "sky", [(i, (i + 1) % n) for i in range(n)])
    down = lax.ppermute(main[:, :4], "sky", [((i + 1) % n, i) for i in range(n)])
    none = jnp.zeros_like(up)
    return main, jnp.concatenate([none, up, down, none], axis=1).reshape(64, WIN)


def body(potential_stock, plane_pick, col_shift, mirror, subcell, lens_weight):
    me = lax.axis_index("real")
    info = jnp.stack([me // 2, me % 2]).astype(I32)
    shift, flip = col_shift[0], mirror[0]
    start = jnp.where(flip == 1, BAND - 4 - 2168 - shift, shift - 4) & (BAND - 1)
    first, rest = start // 128, start % 128

    pair = jnp.concatenate([first, swap(first)])
    quad = jnp.concatenate([pair, lax.ppermute(pair, "real", z_pairs())])
    tins = [quad] + [lax.ppermute(quad, "real", y_pairs(i)) for i in range(1, 4)]
    mate = swap(potential_stock)
    half = halves(1, info, plane_pick, potential_stock, mate)

    chips = plane_pick // 4
    chip_most = jnp.max(jnp.sum((chips[:, None] == chips[None, :]).astype(I32), axis=1))
    upper = jnp.sum(plane_pick // 16)
    half_most = jnp.maximum(upper, PLANES - upper)
    few = jnp.where(chip_most == 2, 2, jnp.where(half_most <= 2, 0, 1))
    branch = jnp.where((chip_most > 2) | (half_most > 3), 3, few).astype(I32)
    main, halo = lax.switch(
        branch,
        [functools.partial(exchange, *case) for case in ((1, 2), (1, 3), (2, 3))] + [any_picks],
        info, plane_pick, first, tins, potential_stock, mate, half,
    )
    return tuple(rays(jnp.concatenate([rest, flip]), subcell.reshape(-1), lens_weight, main, halo))


def solution(mesh):
    return jax.shard_map(
        body,
        mesh=mesh,
        in_specs=(
            P("real", "sky", None),
            P(),
            P("real", None),
            P("real", None),
            P("sky", None),
            P(),
        ),
        out_specs=(P(None, "real", "sky", None), P(None, "real", "sky", None)),
        check_vma=False,
    )
```

```python
import functools

import jax
import jax.numpy as jnp
import numpy as np
from jax import lax
from jax.experimental import pallas as pl
from jax.experimental.pallas import tpu as pltpu
from jax.sharding import PartitionSpec as P

PLANES = 4
ROWS = 32
HALF = 16
TILES = 16
BAND = 16384
WIN = 18 * 128
SCALE = 12288
GROUP = 8
UNROLL = 16

BF = jnp.bfloat16
F32 = jnp.float32
I32 = jnp.int32


def cubic_ints(n):
    return (
        -(n**3) + 16 * n**2 - 64 * n,
        3 * n**3 - 40 * n**2 + 1024,
        -3 * n**3 + 32 * n**2 + 64 * n,
        n**3 - 8 * n**2,
    )


def filters_1d():
    first = {-2: 1, -1: -8, 1: 8, 2: -1}
    second = {-2: -1, -1: 16, 0: -30, 1: 16, 2: -1}
    out = np.zeros((4, 3, 8), np.int64)
    for f in range(4):
        ints = cubic_ints(2 * f + 1)
        for b, w in zip(range(-1, 3), ints):
            out[f, 0, b + 3] += 12 * w
            for d, v in first.items():
                out[f, 1, b + d + 3] += v * w
            for d, v in second.items():
                out[f, 2, b + d + 3] += v * w
    return out


def x_matrix():
    taps = filters_1d()
    full = np.zeros((2, 128, 12 * 64), np.float64)
    for h in range(2):
        for f in range(4):
            for q in range(3):
                block = ((f // 2) * 3 + q) * 2 + (f + h) % 2
                for n in range(8):
                    for j in range(64):
                        full[h, j + 1 + n, block * 64 + j] = taps[f, q, n]
    high = full.astype(jnp.bfloat16).astype(np.float64)
    low = full - high
    assert np.array_equal(low.astype(jnp.bfloat16).astype(np.float64), low)
    return np.concatenate([high, low], axis=1).astype(jnp.bfloat16)


def y_table():
    taps = filters_1d().astype(np.float64) / (float(SCALE) * float(SCALE))
    return taps.astype(np.float32).reshape(-1)


def edge_rows():
    s = np.zeros((2, 32, 128), np.float32)
    for c in range(2):
        for part in range(2 * PLANES):
            for q in range(4):
                s[c, 4 * part + q, 16 * part + 12 * c + q] = 1
    return s.astype(jnp.bfloat16)


def halo_rows():
    s = np.zeros((2, 64, 64), np.float32)
    for p in range(PLANES):
        for q in range(4):
            for c in range(2):
                received, swapped = 4 * p + q, 48 + 4 * p + q
                above, below = (swapped, received) if c == 0 else (received, swapped)
                s[c, 16 * p + 4 + q, above] = 1
                s[c, 16 * p + 8 + q, below] = 1
    return s.astype(jnp.bfloat16)


def slot_planes(pick_ref, chip, slots):
    planes = [jnp.int32(-1)] * slots
    count = jnp.int32(0)
    for p in range(PLANES):
        mine = pick_ref[p] // 4 == chip
        for j in range(slots):
            planes[j] = jnp.where(mine & (count == j), p, planes[j])
        count = count + mine.astype(I32)
    return planes


def half_kernel(slots, info, pick, own, mate, out, sem):
    chip, core = info[0], info[1]
    planes = slot_planes(pick, chip, slots)
    rows = pl.ds(pl.multiple_of(core * HALF, HALF), HALF)
    for j in range(slots):
        entry = pick[jnp.maximum(planes[j], 0)]
        here = (planes[j] < 0) | ((entry // 2) % 2 == core)

        @pl.when(here)
        def _():
            pltpu.make_async_copy(own.at[entry % 2, rows], out.at[j], sem.at[j]).start()

        @pl.when(jnp.logical_not(here))
        def _():
            pltpu.make_async_copy(mate.at[entry % 2, rows], out.at[j], sem.at[j]).start()

    for j in range(slots):
        pltpu.make_async_copy(own.at[0, rows], out.at[j], sem.at[j]).wait()


def cut_kernel(slots, far, info, pick, t0, t1, t2, t3, band, o0, o1, o2, o3, ext, sem_in, sem_out):
    chip = (info[0] + 4 * far) % 8
    planes = slot_planes(pick, chip, slots)
    tins = (t0, t1, t2, t3)
    outs = (o0, o1, o2, o3)
    fetches = []
    for j in range(slots):
        fetches.append((
            pltpu.make_async_copy(band.at[j], ext.at[j, :, pl.ds(0, BAND)], sem_in.at[j, 0]),
            pltpu.make_async_copy(band.at[j, :, pl.ds(0, WIN)], ext.at[j, :, pl.ds(BAND, WIN)], sem_in.at[j, 1]),
        ))
        for copy in fetches[j]:
            copy.start()
    copies = []
    for j in range(slots):
        for copy in fetches[j]:
            copy.wait()
        plane = jnp.maximum(planes[j], 0)
        for i in range(4):
            for e in range(2):
                tile = tins[(4 - i) % 4][e * PLANES + plane] & 127
                start = pl.multiple_of(tile * 128, 128)
                copy = pltpu.make_async_copy(
                    ext.at[j, :, pl.ds(start, WIN)], outs[i].at[e, j], sem_out.at[j, 2 * i + e]
                )
                copy.start()
                copies.append(copy)
    for copy in copies:
        copy.wait()


def select_kernel(slots, info, pick, s_ref, *refs):
    near, far = refs[:4], refs[4:8]
    parts, edges, sem = refs[8:]
    chip, core = info[0], info[1]
    zhi, y = chip // 4, chip % 4
    for p in range(PLANES):
        rank = jnp.int32(0)
        for q in range(p):
            rank = rank + (pick[q] // 4 == pick[p] // 4).astype(I32)
        rank = rank if slots > 1 else 0
        owner = pick[p] // 4
        step = (y - owner % 4 + 4) % 4
        same = owner // 4 == zhi
        for i in range(4):
            for group, here in ((near, same), (far, jnp.logical_not(same))):

                @pl.when(here & (step == i))
                def _():
                    for e in range(2):
                        pltpu.make_async_copy(group[i].at[e, rank], parts.at[e, p], sem.at[e, p]).start()

    for p in range(PLANES):
        for e in range(2):
            pltpu.make_async_copy(near[0].at[0, 0], parts.at[e, p], sem.at[e, p]).wait()
    rows = parts[...].reshape(2 * PLANES * HALF, WIN)
    edges[...] = jnp.dot(s_ref[core], rows, preferred_element_type=F32).astype(BF)


def ray_kernel(
    geo, sub, lens, ytab, halo_ref, mine, swapped, got, got_swapped, w_hbm, deflect_hbm, distort_hbm,
    deflect, distort, w_ref, view, field, sem, sem_out
):
    weights = pltpu.make_async_copy(w_hbm, w_ref, sem)
    weights.start()
    lane = lax.broadcasted_iota(I32, (16, 128), 1)
    left = lax.broadcasted_iota(I32, (1, 1, 128), 2) < 64
    core = geo[2 * PLANES]
    edge = jnp.concatenate([got[...], got_swapped[...]], axis=0)

    def plane(k, carry):
        rest, flip = geo[k], geo[PLANES + k]
        index = jnp.where(flip == 1, rest + 127 - lane, rest + lane)
        low = index < 128
        index = index & 127
        hrow = jnp.dot(halo_ref[core, pl.ds(pl.multiple_of(16 * k, 16), 16), :], edge, preferred_element_type=F32)

        def moved(b):
            cols = pl.ds(b * 128, 128)
            m, w = mine[0, k, :, cols], swapped[0, k, :, cols]
            parts = [jnp.where(core == 0, m, w).astype(F32), jnp.where(core == 0, w, m).astype(F32)]
            parts.append(hrow[:, b * 128 : b * 128 + 128])
            return [jnp.take_along_axis(x, index, axis=1, mode="promise_in_bounds") for x in parts]

        before = moved(0)
        for b in range(17):
            after = moved(b + 1)
            c = jnp.where(flip == 1, 16 - b, b)
            for h in range(3):
                view[0, c, pl.ds(16 * h, 16), :] = jnp.where(low, before[h], after[h]).astype(BF)
            before = after
        for c in range(TILES):
            view[1, c] = jnp.concatenate([view[0, c, :, 64:], view[0, c + 1, :, :64]], axis=1)

        for g in range(TILES // GROUP):
            cs = pl.ds(g * GROUP, GROUP)
            for n in range(3):
                res = []
                for h in range(2):
                    lhs = view[h, cs].reshape(48 * GROUP, 128)
                    lhs = jnp.concatenate([lhs, lhs], axis=1)
                    out = jnp.dot(lhs, w_ref[h, :, pl.ds(n * 256, 256)], preferred_element_type=F32)
                    res.append(out.reshape(GROUP, 48, 256))
                for m in range(2):
                    pair, q = divmod(2 * n + m, 3)
                    r0, r1 = [r[:, :, m * 128 : m * 128 + 128] for r in res]
                    turned = pltpu.roll(jnp.where(left, r1, r0), 64, 2)
                    for fx, part in ((2 * pair, jnp.where(left, r0, r1)), (2 * pair + 1, turned)):
                        field[k, fx, q, cs, pl.ds(8, 32), :] = part[:, :32]
                        field[k, fx, q, cs, pl.ds(0, 8), :] = part[:, 32:40]
                        field[k, fx, q, cs, pl.ds(40, 8), :] = part[:, 40:48]
        return carry

    weights.wait()
    lax.fori_loop(0, PLANES, plane, 0)

    copies = []
    for t in range(4):

        def tile(c, carry):
            o = sub[t * TILES + c]
            fx, fy = o % 4, o // 4
            wy = [[ytab[fy * 24 + q * 8 + n] for n in range(8)] for q in range(3)]
            one = jnp.ones((8, 128), F32)
            zero = jnp.zeros((8, 128), F32)
            dx, dy, a11, a12, a21, a22 = zero, zero, one, zero, zero, one
            for k in range(PLANES):

                def taps(q, lo, hi):
                    return {n: field[k, fx, q, c, pl.ds(8 * t + 5 + n, 8), :] for n in range(lo, hi)}

                def filt(vals, q, lo, hi):
                    terms = [wy[q][n] * vals[n] for n in range(lo, hi)]
                    while len(terms) > 1:
                        odd = [terms[-1]] if len(terms) % 2 else []
                        terms = [a + b for a, b in zip(terms[::2], terms[1::2])] + odd
                    return terms[0]

                s = lens[k]
                v1 = taps(1, 0, 8)
                gx = filt(v1, 0, 2, 6)
                hxy = filt(v1, 1, 0, 8) * s
                v0 = taps(0, 0, 8)
                gy = filt(v0, 1, 0, 8)
                hyy = filt(v0, 2, 0, 8) * s
                v2 = taps(2, 2, 6)
                hxx = filt(v2, 0, 2, 6) * s
                dx = dx + s * gx
                dy = dy + s * gy
                b11 = a11 - (hxx * a11 + hxy * a21)
                b12 = a12 - (hxx * a12 + hxy * a22)
                b21 = a21 - (hxy * a11 + hyy * a21)
                b22 = a22 - (hxy * a12 + hyy * a22)
                a11, a12, a21, a22 = b11, b12, b21, b22
            cols = pl.ds(pl.multiple_of(c * 128, 128), 128)
            rows = pl.ds(8 * t, 8)
            outs = (dx, dy, a11, a12, a21, a22)
            for j in range(2):
                deflect[j, 0, rows, cols] = outs[j]
            for j in range(4):
                distort[j, 0, rows, cols] = outs[2 + j]
            return carry

        lax.fori_loop(0, TILES, tile, 0, unroll=UNROLL)
        rows = pl.ds(8 * t, 8)
        for j, (src, dst) in enumerate(((deflect, deflect_hbm), (distort, distort_hbm))):
            copy = pltpu.make_async_copy(src.at[:, :, rows], dst.at[:, :, rows], sem_out.at[t, j])
            copy.start()
            copies.append(copy)
    for copy in copies:
        copy.wait()


SMEM = pl.BlockSpec(memory_space=pltpu.SMEM)
VMEM = pl.BlockSpec(memory_space=pltpu.VMEM)
ANY = pl.BlockSpec(memory_space=pl.ANY)


def real_index(zhi, y, core):
    return (zhi * 4 + y) * 2 + core


def core_pairs():
    return [(r, r ^ 1) for r in range(16)]


def y_pairs(i):
    return [
        (real_index(zhi, y, c), real_index(zhi, (y + i) % 4, c)) for zhi in range(2) for y in range(4) for c in range(2)
    ]


def z_pairs():
    return [(r, (r + 8) % 16) for r in range(16)]


def edge_pairs(n):
    return [(r * n + s, r * n + (s + (1 if r % 2 else n - 1)) % n) for r in range(16) for s in range(n)]


def params(mib):
    return pltpu.CompilerParams(vmem_limit_bytes=mib * 2**20)


def halves(slots, info, pick, own, mate):
    return pl.pallas_call(
        functools.partial(half_kernel, slots),
        out_shape=jax.ShapeDtypeStruct((slots, HALF, BAND), BF),
        in_specs=[SMEM] * 2 + [ANY] * 2,
        out_specs=ANY,
        scratch_shapes=[pltpu.SemaphoreType.DMA((slots,))],
        compiler_params=params(16),
    )(info, pick, own, mate)


def cut(slots, far, info, pick, tins, band):
    win = jax.ShapeDtypeStruct((2, slots, HALF, WIN), BF)
    return pl.pallas_call(
        functools.partial(cut_kernel, slots, far),
        out_shape=[win] * 4,
        in_specs=[SMEM] * 6 + [ANY],
        out_specs=[ANY] * 4,
        scratch_shapes=[
            pltpu.VMEM((slots, HALF, BAND + WIN), BF),
            pltpu.SemaphoreType.DMA((slots, 2)),
            pltpu.SemaphoreType.DMA((slots, 8)),
        ],
        compiler_params=params(16),
    )(info, pick, *tins, band)


def select(slots, info, pick, near, far):
    return pl.pallas_call(
        functools.partial(select_kernel, slots),
        out_shape=[
            jax.ShapeDtypeStruct((2, PLANES, HALF, WIN), BF),
            jax.ShapeDtypeStruct((32, WIN), BF),
        ],
        in_specs=[SMEM] * 2 + [VMEM] + [ANY] * 8,
        out_specs=[VMEM] * 2,
        scratch_shapes=[pltpu.SemaphoreType.DMA((2, PLANES))],
        compiler_params=params(16),
    )(info, pick, jnp.asarray(edge_rows()), *near, *far)


def part_of(e):
    return pl.BlockSpec((1, PLANES, HALF, WIN), lambda i: (e, 0, 0, 0))


def rays(geo, sub, lens, mine, swapped, got, got_swapped):
    return pl.pallas_call(
        ray_kernel,
        out_shape=[
            jax.ShapeDtypeStruct((2, 1, ROWS, TILES * 128), F32),
            jax.ShapeDtypeStruct((4, 1, ROWS, TILES * 128), F32),
        ],
        grid=(1,),
        in_specs=[SMEM] * 4 + [VMEM, part_of(0), part_of(1), VMEM, VMEM, ANY],
        out_specs=[ANY] * 2,
        scratch_shapes=[
            pltpu.VMEM((2, 1, ROWS, TILES * 128), F32),
            pltpu.VMEM((4, 1, ROWS, TILES * 128), F32),
            pltpu.VMEM((2, 256, 12 * 64), BF),
            pltpu.VMEM((2, 17, 48, 128), BF),
            pltpu.VMEM((PLANES, 4, 3, TILES, 48, 128), F32),
            pltpu.SemaphoreType.DMA,
            pltpu.SemaphoreType.DMA((4, 2)),
        ],
        compiler_params=params(48),
    )(
        geo, sub, lens, jnp.asarray(y_table()), jnp.asarray(halo_rows()),
        mine, swapped, got, got_swapped, jnp.asarray(x_matrix()),
    )


def round_y(outs):
    return [outs[0]] + [lax.ppermute(outs[i], "real", y_pairs(i)) for i in range(1, 4)]


def exchange(slots, info, pick, pair, own, mate, half):
    if slots > 1:
        half = halves(slots, info, pick, own, mate)
    other = lax.ppermute(half, "real", z_pairs())
    tins = [pair] + [lax.ppermute(pair, "real", y_pairs(i)) for i in range(1, 4)]
    near = round_y(cut(slots, 0, info, pick, tins, half))
    far = round_y(cut(slots, 1, info, pick, tins, other))
    return tuple(select(slots, info, pick, near, far))


def body(potential_stock, plane_pick, col_shift, mirror, subcell, lens_weight):
    me = lax.axis_index("real")
    info = jnp.stack([me // 2, me % 2]).astype(I32)
    shift, flip = col_shift[0], mirror[0]
    start = jnp.where(flip == 1, BAND - 4 - 2168 - shift, shift - 4) & (BAND - 1)
    first, rest = start // 128, start % 128

    mate = lax.ppermute(potential_stock, "real", core_pairs())
    pair = jnp.concatenate([first, lax.ppermute(first, "real", core_pairs())])
    half = halves(1, info, plane_pick, potential_stock, mate)

    chips = plane_pick // 4
    most = jnp.max(jnp.sum((chips[:, None] == chips[None, :]).astype(I32), axis=1))
    branch = jnp.where(most <= 1, 0, jnp.where(most <= 2, 1, 2)).astype(I32)
    parts, edges = lax.switch(
        branch,
        [functools.partial(exchange, k) for k in (1, 2, 4)],
        info, plane_pick, pair, potential_stock, mate, half,
    )
    got = lax.ppermute(edges, ("real", "sky"), edge_pairs(lax.axis_size("sky")))
    swapped = lax.ppermute(parts, "real", core_pairs())
    got_swapped = lax.ppermute(got, "real", core_pairs())
    geo = jnp.concatenate([rest, flip, info[1:]])
    return tuple(rays(geo, subcell.reshape(-1), lens_weight, parts, swapped, got, got_swapped))


def solution(mesh):
    return jax.shard_map(
        body,
        mesh=mesh,
        in_specs=(
            P("real", "sky", None),
            P(),
            P("real", None),
            P("real", None),
            P("sky", None),
            P(),
        ),
        out_specs=(P(None, "real", "sky", None), P(None, "real", "sky", None)),
        check_vma=False,
    )
```
